32 devices in a mesh: row: 4 (over y, x), col: 8 (over z, core).
Axes of the slice: x: 2, y: 2, z: 4, core: 2. Of those that a mesh axis runs over, the one named last changes fastest.
Arguments:
- step_index: int32 [2], replicated, may hold values from 50 to 899
- coarse_state: float32 [8, 128, 1024], P(None, 'row', 'col'), may hold values from -6 to 6
- coarse_forcing: bfloat16 [8, 128, 1024], P(None, 'row', 'col'), may hold values from -6 to 6
- fine_state: float32 [8, 512, 4096], P(None, ('row', 'col')), may hold values from -6 to 6
- land_mask: int32 [512, 4096], P(('row', 'col')), may hold values 0 or 1
- inlet_one: bfloat16 [3, 3, 128, 16], replicated, may hold values from -0.5 to 0.5
- timing_one: bfloat16 [128, 128], replicated, may hold values from -0.5 to 0.5
- scale_one: float32 [128], replicated, may hold values from 0.1 to 1.9
- middle_one: bfloat16 [3, 3, 128, 128], replicated, may hold values from -0.1875 to 0.1875
- outlet_one: bfloat16 [3, 3, 8, 128], replicated, may hold values from -0.1875 to 0.1875
- inlet_two: bfloat16 [3, 3, 32, 17], replicated, may hold values from -0.5 to 0.5
- timing_two: bfloat16 [128, 32], replicated, may hold values from -0.5 to 0.5
- land_bias: float32 [32], replicated, may hold values from -4 to 4
- middle_two: bfloat16 [3, 3, 32, 32], replicated, may hold values from -0.375 to 0.375
- outlet_two: bfloat16 [3, 3, 8, 32], replicated, may hold values from -0.375 to 0.375
Outputs:
- coarse_next: float32 [8, 128, 1024], P(None, 'row', 'col')
- noise_one: float32 [8, 128, 1024], P(None, 'row', 'col')
- fine_next: float32 [8, 512, 4096], P(None, ('row', 'col'))
- noise_two: float32 [8, 512, 4096], P(None, ('row', 'col'))
The draws below stay inside these ranges and needn't reach their ends.
Inputs may be any that keep to these rules, and one draw needn't show every extreme that they name: `step_index`: the first entry is the step of the 3 km section, the second that of the 750 m section. `land_mask`: 1 on land, 0 on sea.
All inputs are finite; a program needn't handle non-finite values. No bound on the sum of `land_mask` on one device may be relied on, other than what follows from the above.
Results may differ from the reference program's by a relative error of at most 0.0095.
Values may be sent and summed in bfloat16 or wider, within the bound.
No kernel may reach another device: no remote copies, remote signals or barrier semaphores. Data moves between devices by JAX's collectives and lax.ppermute only.
A program may use at most 192 MiB of HBM per device.

```python
import math
import jax
import jax.numpy as jnp
from jax import lax

FIELDS = 8
HIDDEN_ONE = 128
HIDDEN_TWO = 32
EMBED = 128
COARSE_Y = 128
COARSE_X = 1024
FINE_Y = 512
FINE_X = 4096
BAND = 16


def touch_ends(result, rng, low, top_value):
    longest = result.shape.index(max(result.shape))
    spots = []
    for shift in (0, 1):
        where = [jax.random.randint(jax.random.fold_in(rng, axis), (), 0, length) for axis, length in enumerate(result.shape)]
        where[longest] = (where[longest] + shift) % result.shape[longest]
        spots.append(tuple(where))
    return result.at[spots[0]].set(low).at[spots[1]].set(top_value)


def block_levels(key, dims, cuts, smallest, largest):
    level = 1.0
    for dim, shards_of in cuts:
        draws = jax.random.uniform(jax.random.fold_in(jax.random.fold_in(key, 6), dim), (shards_of,), jnp.float32, smallest / len(cuts), largest / len(cuts))
        level = level * jnp.repeat(jnp.exp(draws), dims[dim] // shards_of).reshape((-1,) + (1,) * (len(dims) - 1 - dim))
    return level


def centred(rng, extent, spread, reach, cuts=(), held_as=jnp.bfloat16):
    factor_of = block_levels(rng, extent, cuts, -0.22, 0.18) if cuts else 1.0
    array = jax.random.normal(rng, extent, jnp.float32) * spread * factor_of
    return jnp.minimum(jnp.maximum(array, -reach), reach).astype(held_as)


def setup_inputs(seed: int = 0) -> dict:
    key_list = jax.random.split(jax.random.key(seed), 16)
    step_index = jax.random.randint(key_list[0], (2,), 50, 900).astype(jnp.int32)
    coarse_state = centred(key_list[1], (FIELDS, COARSE_Y, COARSE_X), 1.0, 6.0, ((1, 4), (2, 8)), jnp.float32)
    coarse_forcing = centred(key_list[2], (FIELDS, COARSE_Y, COARSE_X), 1.0, 6.0, ((1, 4), (2, 8)))
    fine_state = centred(key_list[3], (FIELDS, FINE_Y, FINE_X), 1.0, 6.0, ((1, 32),), jnp.float32)
    land_mask = touch_ends((jax.random.randint(key_list[4], (FINE_Y, FINE_X), 0, 3) < 1).astype(jnp.int32), jax.random.fold_in(key_list[4], 1), 0, 1)
    inlet_one = centred(key_list[5], (3, 3, HIDDEN_ONE, 2 * FIELDS), (18 * FIELDS) ** -0.5, 0.5)
    timing_one = centred(key_list[6], (EMBED, HIDDEN_ONE), EMBED ** -0.5, 0.5)
    scale_one = jnp.clip(1.0 + 0.18 * jax.random.normal(key_list[7], (HIDDEN_ONE,), jnp.float32), 0.1, 1.9)
    middle_one = centred(key_list[8], (3, 3, HIDDEN_ONE, HIDDEN_ONE), (9 * HIDDEN_ONE) ** -0.5, 0.1875)
    outlet_one = centred(key_list[9], (3, 3, FIELDS, HIDDEN_ONE), (9 * HIDDEN_ONE) ** -0.5, 0.1875)
    inlet_two = centred(key_list[10], (3, 3, HIDDEN_TWO, 2 * FIELDS + 1), (18 * FIELDS + 9) ** -0.5, 0.5)
    timing_two = centred(key_list[11], (EMBED, HIDDEN_TWO), EMBED ** -0.5, 0.5)
    land_bias = centred(key_list[12], (HIDDEN_TWO,), 1.0, 4.0, (), jnp.float32)
    middle_two = centred(key_list[13], (3, 3, HIDDEN_TWO, HIDDEN_TWO), (9 * HIDDEN_TWO) ** -0.5, 0.375)
    outlet_two = centred(key_list[14], (3, 3, FIELDS, HIDDEN_TWO), (9 * HIDDEN_TWO) ** -0.5, 0.375)
    return dict(step_index=step_index, coarse_state=coarse_state, coarse_forcing=coarse_forcing, fine_state=fine_state, land_mask=land_mask, inlet_one=inlet_one, timing_one=timing_one, scale_one=scale_one, middle_one=middle_one, outlet_one=outlet_one, inlet_two=inlet_two, timing_two=timing_two, land_bias=land_bias, middle_two=middle_two, outlet_two=outlet_two)


def alpha_bar(moment):
    return jnp.cos((moment / 1000.0 + 0.008) / 1.008 * (math.pi / 2.0)) ** 2

def plan(step_value):
    current_time = step_value.astype(jnp.float32)
    current = alpha_bar(current_time)
    earlier = alpha_bar(current_time - 50.0)
    keeping = jnp.sqrt(earlier / current)
    blending = jnp.sqrt(1.0 - earlier) - jnp.sqrt(earlier) * jnp.sqrt(1.0 - current) / jnp.sqrt(current)
    return (keeping, blending)

def embedding(step_value, timing):
    half_width = timing.shape[0] // 2
    ladder = jnp.arange(half_width, dtype=jnp.float32)
    frequency = jnp.exp(-math.log(10000.0) * ladder / float(half_width))
    angles = step_value.astype(jnp.float32) * frequency
    feature = jnp.concatenate([jnp.sin(angles), jnp.cos(angles)])
    return jnp.dot(feature[None, :], timing.astype(jnp.float32), precision=lax.Precision.HIGHEST)[0]

def conv_valid(padded, weight):
    in_chan = padded.shape[0]
    out_rows = padded.shape[1] - 2
    out_cols = padded.shape[2] - 2
    out_chan = weight.shape[2]
    stacked = jnp.concatenate([padded[:, :, offset:offset + out_cols] for offset in range(3)], axis=0)
    accumulated = jnp.zeros((out_chan, out_rows * out_cols), jnp.float32)
    for offset in range(3):
        tap_matrix = jnp.transpose(weight[offset], (1, 0, 2)).reshape(out_chan, 3 * in_chan)
        window = stacked[:, offset:offset + out_rows, :].reshape(3 * in_chan, out_rows * out_cols)
        accumulated = accumulated + jnp.dot(tap_matrix, window, preferred_element_type=jnp.float32)
    return accumulated.reshape(out_chan, out_rows, out_cols)

def pad_cols(values):
    return jnp.pad(values, ((0, 0), (0, 0), (1, 1)))

def pad_both(values):
    return jnp.pad(values, ((0, 0), (1, 1), (1, 1)))

def normalize(hidden, scale):
    values = hidden.astype(jnp.float32)
    mean_square = lax.optimization_barrier(jnp.mean(values * values, axis=0, keepdims=True))
    return jax.nn.silu(values * lax.rsqrt(mean_square + 1e-06) * scale[:, None, None]).astype(jnp.bfloat16)

def refine(values, axis):
    count = values.shape[axis] - 2
    before = lax.slice_in_dim(values, 0, count, axis=axis)
    middle = lax.slice_in_dim(values, 1, count + 1, axis=axis)
    after = lax.slice_in_dim(values, 2, count + 2, axis=axis)
    pieces = [0.375 * before + 0.625 * middle, 0.125 * before + 0.875 * middle, 0.875 * middle + 0.125 * after, 0.625 * middle + 0.375 * after]
    stacked = jnp.stack(pieces, axis=axis + 1)
    shape = values.shape[:axis] + (4 * count,) + values.shape[axis + 1:]
    return stacked.reshape(shape)

def fine_block(padded, start, total, inlet, middle, outlet, bias_vec, land_bias):
    band_rows = padded.shape[1] - 6

    def inside(margin):
        rows_global = start - margin + jnp.arange(band_rows + 2 * margin, dtype=jnp.int32)
        return ((rows_global >= 0) & (rows_global < total)).astype(jnp.float32)[None, :, None]
    land_float = padded[-1, 1:-1, :].astype(jnp.float32)
    before_act = conv_valid(pad_cols(padded), inlet) + bias_vec[:, None, None] + land_bias[:, None, None] * land_float[None]
    hidden = (jax.nn.silu(before_act) * inside(2)).astype(jnp.bfloat16)
    summed = ((hidden[:, 1:-1, :].astype(jnp.float32) + conv_valid(pad_cols(hidden), middle)) * inside(1)).astype(jnp.bfloat16)
    return conv_valid(pad_cols(summed), outlet)

def reference(step_index, coarse_state, coarse_forcing, fine_state, land_mask, inlet_one, timing_one, scale_one, middle_one, outlet_one, inlet_two, timing_two, land_bias, middle_two, outlet_two):
    keep_one, blend_one = plan(step_index[0])
    keep_two, blend_two = plan(step_index[1])
    coarse_input = jnp.concatenate([coarse_state.astype(jnp.bfloat16), coarse_forcing], axis=0)
    bias_one = embedding(step_index[0], timing_one)
    hidden_one = jax.nn.silu(conv_valid(pad_both(coarse_input), inlet_one) + bias_one[:, None, None]).astype(jnp.bfloat16)
    active_one = normalize(hidden_one, scale_one)
    summed_one = (hidden_one.astype(jnp.float32) + conv_valid(pad_both(active_one), middle_one)).astype(jnp.bfloat16)
    noise_one = conv_valid(pad_both(summed_one), outlet_one)
    coarse_next = keep_one * coarse_state + blend_one * noise_one
    vertical = refine(jnp.pad(coarse_next, ((0, 0), (1, 1), (0, 0)), mode='edge'), 1)
    lifted = refine(jnp.pad(vertical, ((0, 0), (0, 0), (1, 1)), mode='edge'), 2)
    fine_input = jnp.concatenate([fine_state.astype(jnp.bfloat16), lifted.astype(jnp.bfloat16), land_mask.astype(jnp.bfloat16)[None]], axis=0)
    bias_two = embedding(step_index[1], timing_two)
    padded = jnp.pad(fine_input, ((0, 0), (3, 3), (0, 0)))
    block_count = FINE_Y // BAND

    def one_block(block_id):
        start = (block_id * BAND).astype(jnp.int32)
        piece = lax.dynamic_slice_in_dim(padded, start, BAND + 6, 1)
        return fine_block(piece, start, FINE_Y, inlet_two, middle_two, outlet_two, bias_two, land_bias)
    blocks = lax.map(one_block, jnp.arange(block_count, dtype=jnp.int32))
    noise_two = jnp.transpose(blocks, (1, 0, 2, 3)).reshape(FIELDS, FINE_Y, FINE_X)
    fine_next = keep_two * fine_state + blend_two * noise_two
    return (coarse_next, noise_one, fine_next, noise_two)
```

```python
import functools
import math

import jax
import jax.numpy as jnp
import numpy as np
from jax import lax
from jax.experimental import pallas as pl
from jax.experimental.pallas import tpu as pltpu
from jax.sharding import PartitionSpec as P

BF = jnp.bfloat16
F32 = jnp.float32
VMEM = pl.BlockSpec(memory_space=pltpu.VMEM)
SMEM = pl.BlockSpec(memory_space=pltpu.SMEM)
EDGE = 16
ROWS1 = 5
ROWS2 = 6
ROWS3 = 8
LANES = 128


def params(mib):
    return pltpu.CompilerParams(vmem_limit_bytes=mib << 20)


def silu(v):
    return v * (0.5 * jnp.tanh(0.5 * v) + 0.5)


def starts_of(rows, height):
    return [min(s, rows - height) for s in range(0, rows, height)]


def shift_pairs(count, by):
    return [(i, i + by) for i in range(count) if 0 <= i + by < count]


def alpha_bar(moment):
    return jnp.cos((moment / 1000.0 + 0.008) / 1.008 * (math.pi / 2.0)) ** 2


def plan(step_value):
    current_time = step_value.astype(F32)
    current = alpha_bar(current_time)
    earlier = alpha_bar(current_time - 50.0)
    keeping = jnp.sqrt(earlier / current)
    blending = jnp.sqrt(1.0 - earlier) - jnp.sqrt(earlier) * jnp.sqrt(1.0 - current) / jnp.sqrt(
        current
    )
    return (keeping, blending)


def embedding(step_value, timing):
    half_width = timing.shape[0] // 2
    ladder = jnp.arange(half_width, dtype=F32)
    frequency = jnp.exp(-math.log(10000.0) * ladder / float(half_width))
    angles = step_value.astype(F32) * frequency
    feature = jnp.concatenate([jnp.sin(angles), jnp.cos(angles)])
    return jnp.dot(feature[None, :], timing.astype(F32), precision=lax.Precision.HIGHEST)[0]


def pack_kernel(tile_rows, chunk, state, forcing, fine, land, pick, comb, to_next, to_prev, wide):
    wide[...] = forcing[...].astype(F32)
    for y in range(tile_rows):
        comb[y] = jnp.concatenate(
            [state[pl.ds(y, 8, stride=tile_rows), :], wide[pl.ds(y, 8, stride=tile_rows), :]], axis=0
        ).astype(BF)
    for c in range(0, fine.shape[1], chunk):
        cols = slice(c, c + chunk)
        operand = jnp.concatenate([fine[:, cols], land[:, cols].astype(F32)], axis=0).astype(BF)
        made = jnp.dot(pick[...], operand, preferred_element_type=F32).astype(BF)
        to_next[:, cols] = made[0:32]
        to_prev[:, cols] = made[32:64]


def weight_kernel(
    band, inlet_one, middle_one, outlet_one, inlet_two, middle_two, outlet_two, bias_two, land_bias,
    first_one, mid_one, last_one, first_two, mid_two, last_two, wide1, wide2, wide3,
):
    first_one[...] = jnp.zeros_like(first_one)
    for dx in range(3):
        for i in range(2):
            for dy in range(3):
                at = 192 + (i + dy) * 16
                first_one[dx, at : at + 16, i * 128 : (i + 1) * 128] = (
                    inlet_one[dy, dx].astype(F32).T.astype(BF)
                )
    mid_one[...] = jnp.zeros_like(mid_one)
    last_one[...] = jnp.zeros_like(last_one)
    for dx in range(3):
        for dy in range(3):
            turned = middle_one[dy, dx].astype(F32).T.astype(BF)
            for i in range(2):
                at = dx * 512 + (i + dy) * 128
                mid_one[at : at + 128, i * 128 : (i + 1) * 128] = turned
    for dx in range(3):
        for slot in range(2):
            pieces = []
            for i in range(2):
                halves = []
                for par in range(2):
                    dy = 2 * slot + par - i
                    halves.append(
                        outlet_one[dy, dx].astype(F32) if 0 <= dy <= 2 else jnp.zeros((8, 128), F32)
                    )
                pieces.append(jnp.concatenate(halves, axis=1))
            at = dx * 32 + slot * 16
            last_one[at : at + 16, :] = jnp.concatenate(pieces, axis=0).astype(BF)

    wide1[...] = jnp.zeros_like(wide1)
    wide2[...] = jnp.zeros_like(wide2)
    wide3[...] = jnp.zeros_like(wide3)
    span = (ROWS1 + 2) * 16
    for dx in range(3):
        for dy in range(3):
            w1 = inlet_two[dy, dx].astype(F32)[:, :16]
            w2 = middle_two[dy, dx].astype(F32)
            for i in range(ROWS1):
                at = dx * span + (i + dy) * 16
                wide1[32 * i : 32 * i + 32, at : at + 16] = w1
            for i in range(ROWS2):
                at = dx * 256 + (i + dy) * 32
                wide2[32 * i : 32 * i + 32, at : at + 32] = w2
    columns = lax.broadcasted_iota(jnp.int32, (ROWS3, 32 * (ROWS3 + 2)), 1)
    offset = columns // 32 - lax.broadcasted_iota(jnp.int32, columns.shape, 0)
    for dx in range(3):
        for o in range(8):
            value = jnp.zeros(columns.shape, F32)
            for dy in range(3):
                line = outlet_two[dy, dx].astype(F32)[o : o + 1]
                line = jnp.concatenate([line] * (ROWS3 + 2), axis=1)
                value = jnp.where(offset == dy, line, value)
            row = (dx * 8 + o) * ROWS3
            wide3[row : row + ROWS3, :] = value
    mid_two[...] = wide2[...].astype(BF)
    last_two[...] = wide3[...].astype(BF)
    lane = lax.broadcasted_iota(jnp.int32, (32, LANES), 1)

    def spread(column):
        return jnp.broadcast_to(column, (32, LANES))

    def split(value):
        high = value.astype(BF).astype(F32)
        return high, (value - high).astype(BF).astype(F32)

    taps = [[spread(inlet_two[dy, dx].astype(F32)[:, 16:17]) for dx in range(3)] for dy in range(3)]
    centre_high, centre_low = split(taps[1][1] + spread(land_bias[...]))
    taps[1][1] = centre_high
    bias_high, bias_low = split(spread(bias_two[...]))
    starts = starts_of(band + 4, ROWS1)
    for b, s in enumerate(starts):
        for i in range(ROWS1):
            value = jnp.where(lane == 32, bias_high, 0.0)
            value = jnp.where(lane == 33, bias_low, value)
            for dx in range(3):
                for dy in range(3):
                    value = jnp.where(lane == dx * 32 + 5 + s + i + dy, taps[dy][dx], value)
            value = jnp.where(lane == 96 + 5 + s + i + 1, centre_low, value)
            first_two[b, 32 * i : 32 * i + 32, 0:LANES] = value.astype(BF)
        first_two[b, :, LANES:] = wide1[...].astype(BF)


def coarse_kernel(
    tile_rows, cols, dests, place, rates, own, west, east, state, first_one, mid_one, last_one,
    bias, scale, coarse_next, noise_one, sends, turned, hidden, active, summed, taps,
):
    px = cols + 2 * EDGE
    rows_before, rows_total, cols_before, cols_total = (place[k] for k in range(4))
    keep, blend = rates[0], rates[1]
    ext = tile_rows + 10
    pairs = (tile_rows + 8) // 2
    windows = [min(14 * k, ext - 16) for k in range(-(-pairs // 7))]
    for k, at in enumerate(windows):
        parts = [
            ref[at : at + 16].reshape(256, cols).astype(F32).T for ref in (west, own, east)
        ]
        whole = jnp.concatenate([parts[0][cols - EDGE :], parts[1], parts[2][:EDGE]], axis=0)
        turned[k, 0] = pltpu.roll(whole, 1, 0).astype(BF)
        turned[k, 1] = whole.astype(BF)
        turned[k, 2] = pltpu.roll(whole, px - 1, 0).astype(BF)

    column = cols_before - EDGE + lax.broadcasted_iota(jnp.int32, (px, 256), 0)
    half = lax.broadcasted_iota(jnp.int32, (px, 256), 1) // 128
    inside = jnp.where((column >= 0) & (column < cols_total), 1.0, 0.0)

    def mask(first_row):
        row = rows_before - 5 + first_row + half
        return jnp.where((row >= 0) & (row < rows_total), inside, 0.0)

    for p in range(pairs):
        k = p // 7
        off = 192 - (2 * p - windows[k]) * 16
        acc = jnp.dot(turned[k, 0], first_one[0, off : off + 256], preferred_element_type=F32)
        for dx in (1, 2):
            acc += jnp.dot(turned[k, dx], first_one[dx, off : off + 256], preferred_element_type=F32)
        low = silu(acc + bias[...]).astype(BF)
        hidden[p] = low
        value = low.astype(F32)
        square = value * value
        scaled = []
        for h in range(2):
            mean = jnp.mean(square[:, h * 128 : (h + 1) * 128], axis=1, keepdims=True)
            scaled.append(value[:, h * 128 : (h + 1) * 128] * lax.rsqrt(mean + 1e-06))
        act = silu(jnp.concatenate(scaled, axis=1) * scale[...]) * mask(1 + 2 * p)
        active[p, :, 0:256] = pltpu.roll(act, 1, 0).astype(BF)
        active[p, :, 256:512] = act.astype(BF)
        active[p, :, 512:768] = pltpu.roll(act, px - 1, 0).astype(BF)

    for p in range(pairs - 1):
        acc = None
        for dx in range(3):
            for q in range(2):
                at = dx * 512 + q * 256
                term = jnp.dot(
                    active[p + q, :, dx * 256 : (dx + 1) * 256], mid_one[at : at + 256],
                    preferred_element_type=F32,
                )
                acc = term if acc is None else acc + term
        rest = jnp.concatenate([hidden[p, :, 128:256], hidden[p + 1, :, 0:128]], axis=1)
        summed[p] = ((acc + rest.astype(F32)) * mask(2 + 2 * p)).astype(BF)

    for p in range(pairs - 1):
        taps[p] = lax.dot_general(
            last_one[...], summed[p], (((1,), (1,)), ((), ())), preferred_element_type=F32
        )
    each = tile_rows // dests
    for p in range(pairs - 2):
        noise = None
        for dx in range(3):
            at = EDGE - 1 + dx
            term = (
                taps[p, dx * 32 : dx * 32 + 16, at : at + cols]
                + taps[p + 1, dx * 32 + 16 : dx * 32 + 32, at : at + cols]
            )
            noise = term if noise is None else noise + term
        made = []
        for i in range(2):
            y = 2 * p - 2 + i
            part = noise[8 * i : 8 * i + 8]
            if 0 <= y < tile_rows:
                rows = pl.ds(y, 8, stride=tile_rows)
                after = keep * state[rows, :] + blend * part
                noise_one[rows, :] = part
                coarse_next[rows, :] = after
            else:
                after = keep * own[y + 5].astype(F32)[0:8] + blend * part
            made.append(after)
        made = jnp.concatenate(made, axis=0).astype(BF)
        for d in range(dests):
            slot = 2 * p - each * d
            if 0 <= slot < each + 4:
                sends[d, slot * 8 : slot * 8 + 16, :] = made


def fine_kernel(
    band, width, chunk, place, rates, coarse, fine, land, above, below, spread, order, first_two, mid_two,
    last_two, fine_next, noise_two, lifted, inputs, ground, hidden, summed,
):
    keep, blend = rates[2], rates[3]
    top = jnp.where(place[4] > 0, 1.0, 0.0)
    bottom = jnp.where(place[4] < place[5] - 1, 1.0, 0.0)
    ext = band + 6
    own = band // 4
    sources = width // (4 * LANES)
    zeros = lambda rows: jnp.zeros((rows, LANES), BF)
    for ref in (inputs, ground, hidden, summed):
        ref[:, 0:LANES] = zeros(ref.shape[0])
        ref[:, LANES + width : 2 * LANES + width] = zeros(ref.shape[0])

    for m in range(sources):
        block = coarse[m].astype(F32)
        rows = [block[8 * j : 8 * j + 8] for j in range(own + 4)]
        rows[1] = top * rows[1] + (1.0 - top) * rows[2]
        rows[own + 2] = bottom * rows[own + 2] + (1.0 - bottom) * rows[own + 1]
        made = []
        for e in range(ext):
            k, phase = divmod(e - 3, 4)
            j = k + 2
            other, near, far = (
                (j - 1, 0.625, 0.375), (j - 1, 0.875, 0.125), (j + 1, 0.875, 0.125), (j + 1, 0.625, 0.375),
            )[phase]
            value = near * rows[j] + far * rows[other]
            if e < 3:
                value = value * top
            if e >= band + 3:
                value = value * bottom
            made.append(value)
        made = jnp.concatenate(made, axis=0)
        lifted[:, (m + 1) * LANES : (m + 2) * LANES] = made
        if m == 0:
            lifted[:, 0:LANES] = jnp.broadcast_to(made[:, 0:1], (ext * 8, LANES))
        if m == sources - 1:
            lifted[:, (m + 2) * LANES : (m + 3) * LANES] = jnp.broadcast_to(
                made[:, LANES - 1 : LANES], (ext * 8, LANES)
            )

    lane = lax.broadcasted_iota(jnp.int32, (ext * 8, LANES), 1)
    pad_rows = ground.shape[0] - band - 16

    def fill(m, _):
        c = pl.multiple_of(m * LANES, LANES)
        main = lifted[:, pl.ds(c + LANES, LANES)]
        side = jnp.where(
            lane == LANES - 1, lifted[:, pl.ds(c, LANES)], lifted[:, pl.ds(c + 2 * LANES, LANES)]
        )
        fields = jnp.dot(
            jnp.concatenate([main, side], axis=1).astype(BF), spread[...], preferred_element_type=F32
        )
        x = pl.multiple_of(m * 4 * LANES, LANES)
        cols = pl.ds(x, 4 * LANES)
        upper = above[:, cols].astype(F32)
        lower = below[:, cols].astype(F32)
        held = jnp.dot(order[...], fine[:, cols].astype(BF), preferred_element_type=F32)
        for e in range(ext):
            if e < 3:
                state = upper[8 * e : 8 * e + 8]
            elif e < band + 3:
                state = held[8 * (e - 3) : 8 * (e - 3) + 8]
            else:
                state = lower[8 * (e - band - 3) : 8 * (e - band - 3) + 8]
            inputs[16 * e : 16 * e + 16, pl.ds(x + LANES, 4 * LANES)] = jnp.concatenate(
                [state, fields[8 * e : 8 * e + 8]], axis=0
            ).astype(BF)
        pieces = [upper[24:32], land[:, cols].astype(F32), lower[24:32]]
        if pad_rows:
            pieces.append(jnp.zeros((pad_rows, 4 * LANES), F32))
        covered = jnp.concatenate(pieces, axis=0)
        ground[:, pl.ds(x + LANES, 4 * LANES)] = covered.astype(BF)
        return 0

    lax.fori_loop(0, sources, fill, 0)

    def three(block):
        return [block[:, LANES - 1 + k : LANES - 1 + k + chunk] for k in range(3)]

    ones_row = lax.broadcasted_iota(jnp.int32, (ground.shape[0], chunk), 0) < 2

    def first(n, _):
        c = pl.multiple_of(n * chunk, chunk)
        span = pl.ds(c, chunk + 2 * LANES)
        west, here, east = three(ground[:, span])
        marked = jnp.where(ones_row, 1.0, here.astype(F32)).astype(BF)
        base = [west, marked, east, here]
        for b, s in enumerate(starts_of(band + 4, ROWS1)):
            block = inputs[16 * s : 16 * (s + ROWS1 + 2), span]
            operand = jnp.concatenate(base + three(block), axis=0)
            value = silu(jnp.dot(first_two[b], operand, preferred_element_type=F32))
            for i in range(ROWS1):
                part = value[32 * i : 32 * i + 32]
                if s + i < 2:
                    part = part * top
                if s + i >= band + 2:
                    part = part * bottom
                at = 32 * (s + i)
                hidden[at : at + 32, pl.ds(c + LANES, chunk)] = part.astype(BF)
        return 0

    lax.fori_loop(0, width // chunk, first, 0)

    def second(n, _):
        c = pl.multiple_of(n * chunk, chunk)
        span = pl.ds(c, chunk + 2 * LANES)
        for s in starts_of(band + 2, ROWS2):
            block = hidden[32 * s : 32 * (s + ROWS2 + 2), span]
            value = jnp.dot(
                mid_two[...], jnp.concatenate(three(block), axis=0), preferred_element_type=F32
            )
            for i in range(ROWS2):
                part = value[32 * i : 32 * i + 32] + block[
                    32 * i + 32 : 32 * i + 64, LANES : LANES + chunk
                ].astype(F32)
                if s + i < 1:
                    part = part * top
                if s + i >= band + 1:
                    part = part * bottom
                at = 32 * (s + i)
                summed[at : at + 32, pl.ds(c + LANES, chunk)] = part.astype(BF)
        return 0

    lax.fori_loop(0, width // chunk, second, 0)

    def third(n, _):
        c = pl.multiple_of(n * chunk, chunk)
        cols = pl.ds(c, chunk)
        for s in range(0, band, ROWS3):
            value = jnp.dot(
                last_two[...],
                summed[32 * s : 32 * (s + ROWS3 + 2), pl.ds(c, chunk + 2 * LANES)],
                preferred_element_type=F32,
            )
            high = 8 * ROWS3
            parts = [
                value[k * high : (k + 1) * high, LANES - 1 + k : LANES - 1 + k + chunk] for k in range(3)
            ]
            noise = parts[0] + parts[1] + parts[2]
            for o in range(8):
                rows = slice(o * band + s, o * band + s + ROWS3)
                part = noise[ROWS3 * o : ROWS3 * o + ROWS3]
                noise_two[rows, cols] = part
                fine_next[rows, cols] = keep * fine[rows, cols] + blend * part
        return 0

    lax.fori_loop(0, width // chunk, third, 0)


def spread_matrix():
    near = np.array([0.625, 0.875, 0.875, 0.625])
    far = np.array([0.375, 0.125, 0.125, 0.375])
    made = np.zeros((2 * LANES, 4 * LANES))
    for n in range(4 * LANES):
        k, phase = divmod(n, 4)
        made[k, n] = near[phase]
        other = k - 1 if phase < 2 else k + 1
        if other < 0:
            made[2 * LANES - 1, n] = far[phase]
        elif other == LANES:
            made[LANES, n] = far[phase]
        else:
            made[other, n] = far[phase]
    return jnp.asarray(made, BF)


def order_matrix(band):
    made = np.zeros((8 * band, 8 * band))
    for y in range(band):
        for o in range(8):
            made[8 * y + o, o * band + y] = 1
    return jnp.asarray(made, BF)


def pick_matrix(band):
    made = np.zeros((64, 9 * band))
    for k, (first, low) in enumerate(((band - 3, band - 8), (0, 0))):
        for y in range(3):
            for o in range(8):
                made[32 * k + 8 * y + o, o * band + first + y] = 1
        for y in range(8):
            made[32 * k + 24 + y, 8 * band + low + y] = 1
    return jnp.asarray(made, BF)


def body(
    step_index, coarse_state, coarse_forcing, fine_state, land_mask, inlet_one, timing_one, scale_one,
    middle_one, outlet_one, inlet_two, timing_two, land_bias, middle_two, outlet_two,
):
    fields, tile_rows, cols = coarse_state.shape
    _, band, width = fine_state.shape
    row_count, col_count = lax.axis_size("row"), lax.axis_size("col")
    row_at, col_at = lax.axis_index("row"), lax.axis_index("col")
    count = row_count * col_count
    state = coarse_state.reshape(fields * tile_rows, cols)
    forcing = coarse_forcing.reshape(fields * tile_rows, cols)
    fine = fine_state.reshape(fields * band, width)

    keep_one, blend_one = plan(step_index[0])
    keep_two, blend_two = plan(step_index[1])
    rates = jnp.stack([keep_one, blend_one, keep_two, blend_two])
    bias_one = embedding(step_index[0], timing_one)
    bias_two = embedding(step_index[1], timing_two)
    place = jnp.stack(
        [
            row_at * tile_rows, jnp.int32(row_count * tile_rows), col_at * cols,
            jnp.int32(col_count * cols), row_at * col_count + col_at, jnp.int32(count),
        ]
    ).astype(jnp.int32)

    comb, to_next, to_prev = pl.pallas_call(
        functools.partial(pack_kernel, tile_rows, 1024),
        out_shape=(
            jax.ShapeDtypeStruct((tile_rows, 2 * fields, cols), BF),
            jax.ShapeDtypeStruct((32, width), BF),
            jax.ShapeDtypeStruct((32, width), BF),
        ),
        in_specs=[VMEM] * 5,
        out_specs=[VMEM] * 3,
        scratch_shapes=[pltpu.VMEM((fields * tile_rows, cols), F32)],
        compiler_params=params(24),
        name="pack",
    )(state, forcing, fine, land_mask, pick_matrix(band))

    north = lax.ppermute(comb[tile_rows - 5 :], "row", shift_pairs(row_count, 1))
    south = lax.ppermute(comb[:5], "row", shift_pairs(row_count, -1))
    tall = jnp.concatenate([north, comb, south], axis=0)
    west = lax.ppermute(tall, "col", shift_pairs(col_count, 1))
    east = lax.ppermute(tall, "col", shift_pairs(col_count, -1))
    above = lax.ppermute(to_next, ("row", "col"), shift_pairs(count, 1))
    below = lax.ppermute(to_prev, ("row", "col"), shift_pairs(count, -1))

    blocks = len(starts_of(band + 4, ROWS1))
    deep = LANES + 3 * 16 * (ROWS1 + 2)
    weights = pl.pallas_call(
        functools.partial(weight_kernel, band),
        out_shape=(
            jax.ShapeDtypeStruct((3, 448, 256), BF),
            jax.ShapeDtypeStruct((1536, 256), BF),
            jax.ShapeDtypeStruct((96, 256), BF),
            jax.ShapeDtypeStruct((blocks, 32 * ROWS1, deep), BF),
            jax.ShapeDtypeStruct((32 * ROWS2, 768), BF),
            jax.ShapeDtypeStruct((24 * ROWS3, 32 * (ROWS3 + 2)), BF),
        ),
        in_specs=[VMEM] * 8,
        out_specs=[VMEM] * 6,
        scratch_shapes=[
            pltpu.VMEM((32 * ROWS1, deep - LANES), F32),
            pltpu.VMEM((32 * ROWS2, 768), F32),
            pltpu.VMEM((24 * ROWS3, 32 * (ROWS3 + 2)), F32),
        ],
        compiler_params=params(24),
        name="weights",
    )(
        inlet_one, middle_one, outlet_one, inlet_two, middle_two, outlet_two, bias_two[:, None],
        land_bias[:, None],
    )
    first_one, mid_one, last_one, first_two, mid_two, last_two = weights

    px = cols + 2 * EDGE
    pairs = (tile_rows + 8) // 2
    each = tile_rows // col_count
    coarse_next, noise_one, sends = pl.pallas_call(
        functools.partial(coarse_kernel, tile_rows, cols, col_count),
        out_shape=(
            jax.ShapeDtypeStruct((fields * tile_rows, cols), F32),
            jax.ShapeDtypeStruct((fields * tile_rows, cols), F32),
            jax.ShapeDtypeStruct((col_count, (each + 4) * fields, cols), BF),
        ),
        in_specs=[SMEM] * 2 + [VMEM] * 9,
        out_specs=[VMEM] * 3,
        scratch_shapes=[
            pltpu.VMEM((-(-pairs // 7), 3, px, 256), BF),
            pltpu.VMEM((pairs, px, 256), BF),
            pltpu.VMEM((pairs, px, 768), BF),
            pltpu.VMEM((pairs - 1, px, 256), BF),
            pltpu.VMEM((pairs - 1, 96, px), F32),
        ],
        compiler_params=params(40),
        name="coarse",
    )(
        place, rates, tall, west, east, state, first_one, mid_one, last_one,
        jnp.tile(bias_one, 2)[None, :], jnp.tile(scale_one, 2)[None, :],
    )

    arrived = lax.all_to_all(sends, "col", split_axis=0, concat_axis=0, tiled=True)

    ground_rows = -(-(band + 16) // 32) * 32
    fine_next, noise_two = pl.pallas_call(
        functools.partial(fine_kernel, band, width, 512),
        out_shape=(
            jax.ShapeDtypeStruct((fields * band, width), F32),
            jax.ShapeDtypeStruct((fields * band, width), F32),
        ),
        in_specs=[SMEM] * 2 + [VMEM] * 10,
        out_specs=[VMEM] * 2,
        scratch_shapes=[
            pltpu.VMEM(((band + 6) * 8, width // 4 + 2 * LANES), F32),
            pltpu.VMEM(((band + 6) * 16, width + 2 * LANES), BF),
            pltpu.VMEM((ground_rows, width + 2 * LANES), BF),
            pltpu.VMEM(((band + 4) * 32, width + 2 * LANES), BF),
            pltpu.VMEM(((band + 2) * 32, width + 2 * LANES), BF),
        ],
        compiler_params=params(56),
        name="fine",
    )(
        place, rates, arrived, fine, land_mask, above, below, spread_matrix(), order_matrix(band),
        first_two, mid_two, last_two,
    )

    return (
        coarse_next.reshape(coarse_state.shape),
        noise_one.reshape(coarse_state.shape),
        fine_next.reshape(fine_state.shape),
        noise_two.reshape(fine_state.shape),
    )


def solution(mesh):
    return jax.shard_map(
        body,
        mesh=mesh,
        in_specs=(
            P(), P(None, "row", "col"), P(None, "row", "col"), P(None, ("row", "col"), None),
            P(("row", "col"), None), P(), P(), P(), P(), P(), P(), P(), P(), P(), P(),
        ),
        out_specs=(
            P(None, "row", "col"), P(None, "row", "col"), P(None, ("row", "col"), None),
            P(None, ("row", "col"), None),
        ),
        check_vma=False,
    )
```

```python
import functools
import math

import jax
import jax.numpy as jnp
import numpy as np
from jax import lax
from jax.experimental import pallas as pl
from jax.experimental.pallas import tpu as pltpu
from jax.sharding import PartitionSpec as P

BF = jnp.bfloat16
F32 = jnp.float32
VMEM = pl.BlockSpec(memory_space=pltpu.VMEM)
SMEM = pl.BlockSpec(memory_space=pltpu.SMEM)
ANY = pl.BlockSpec(memory_space=pl.ANY)
WHOLE = pl.BlockSpec()
EDGE = 16
ROWS1 = 6
ROWS2 = 6
ROWS3 = 8
LANES = 128


def params(mib):
    return pltpu.CompilerParams(vmem_limit_bytes=mib << 20)


def silu(v):
    return v * (0.5 * jnp.tanh(0.5 * v) + 0.5)


def starts_of(rows, height):
    return [min(s, rows - height) for s in range(0, rows, height)]


def shift_pairs(count, by):
    return [(i, (i + by) % count) for i in range(count)]


def alpha_bar(moment):
    return jnp.cos((moment / 1000.0 + 0.008) / 1.008 * (math.pi / 2.0)) ** 2


def plan(step, shape):
    current_time = jnp.full(shape, step.astype(F32), F32)
    current = alpha_bar(current_time)
    earlier = alpha_bar(current_time - 50.0)
    keeping = jnp.sqrt(earlier / current)
    blending = jnp.sqrt(1.0 - earlier) - jnp.sqrt(earlier) * jnp.sqrt(1.0 - current) / jnp.sqrt(
        current
    )
    return (keeping, blending)


def embed(step, ladder, timing):
    half = ladder.shape[1] // 2
    angles = step.astype(F32) * ladder[...]
    lane = lax.broadcasted_iota(jnp.int32, angles.shape, 1)
    feature = jnp.where(lane < half, jnp.sin(angles), jnp.cos(angles))
    parts = []
    for _ in range(3):
        part = feature.astype(BF)
        feature = feature - part.astype(F32)
        parts.append(part)
    return sum(jnp.dot(part, timing, preferred_element_type=F32) for part in parts)


def ladder_rows(width):
    steps = np.exp(-math.log(10000.0) * np.arange(width // 2) / (width // 2))
    return jnp.asarray(np.tile(np.concatenate([steps, steps]), (8, 1)), F32)


def pack_kernel(tile_rows, state, forcing, comb, top, bottom, near, wide, narrow, sems):
    copies = [
        pltpu.make_async_copy(state, near, sems.at[0]),
        pltpu.make_async_copy(forcing, narrow, sems.at[1]),
    ]
    for copy in copies:
        copy.start()
    for copy in copies:
        copy.wait()
    wide[...] = narrow[...].astype(F32)
    for y in range(tile_rows):
        made = jnp.concatenate(
            [near[pl.ds(y, 8, stride=tile_rows), :], wide[pl.ds(y, 8, stride=tile_rows), :]], axis=0
        ).astype(BF)
        comb[y] = made
        if y < 5:
            top[y] = made
        if y >= tile_rows - 5:
            bottom[y - tile_rows + 5] = made


def sort_kernel(fine, land, turn, order, own, ground, to_next, to_prev):
    for m in range(fine.shape[1] // (4 * LANES)):
        cols = slice(4 * LANES * m, 4 * LANES * (m + 1))
        block = jnp.concatenate([fine[:, cols], land[:, cols].astype(F32)], axis=0).astype(BF)
        block = jnp.dot(block, turn[...], preferred_element_type=F32).astype(BF)
        made = jnp.dot(order[...], block, preferred_element_type=F32).astype(BF)
        at = slice(m * LANES, (m + 1) * LANES)
        for j in range(4):
            part = made[:, j * LANES : (j + 1) * LANES]
            to_next[j, :, at] = part[0:32]
            to_prev[j, :, at] = part[32:64]
            ground[j, :, at] = part[64:80]
            own[j, :, at] = part[80:]


def ground_row(band, e):
    if e < 3:
        return 21 + e
    return e - 3 if e < band + 3 else 24 + e - band - 3


def coarse_weights(
    steps, ladder, timing, inlet_one, middle_one, outlet_one, first_one, mid_one, last_one, bias,
):
    made = embed(steps[0], ladder, timing[...])
    bias[...] = jnp.concatenate([made, made], axis=1)
    first_one[...] = jnp.zeros_like(first_one)
    for dx in range(3):
        for i in range(2):
            for dy in range(3):
                at = 192 + (i + dy) * 16
                first_one[dx, at : at + 16, i * 128 : (i + 1) * 128] = (
                    inlet_one[dy, dx].astype(F32).T.astype(BF)
                )
    mid_one[...] = jnp.zeros_like(mid_one)
    last_one[...] = jnp.zeros_like(last_one)
    for dx in range(3):
        for dy in range(3):
            turned = middle_one[dy, dx].astype(F32).T.astype(BF)
            for i in range(2):
                at = dx * 512 + (i + dy) * 128
                mid_one[at : at + 128, i * 128 : (i + 1) * 128] = turned
    for dx in range(3):
        for slot in range(2):
            pieces = []
            for i in range(2):
                halves = []
                for par in range(2):
                    dy = 2 * slot + par - i
                    halves.append(
                        outlet_one[dy, dx].astype(F32) if 0 <= dy <= 2 else jnp.zeros((8, 128), F32)
                    )
                pieces.append(jnp.concatenate(halves, axis=1))
            at = dx * 32 + slot * 16
            last_one[at : at + 16, :] = jnp.concatenate(pieces, axis=0).astype(BF)


def fine_weights(
    band, steps, ladder, timing, inlet_two, middle_two, outlet_two, land_bias, first_two, mid_two, last_two,
    wide1, wide2, wide3,
):
    bias_two = embed(steps[1], ladder, timing[...])[0:1].T
    wide1[...] = jnp.zeros_like(wide1)
    wide2[...] = jnp.zeros_like(wide2)
    wide3[...] = jnp.zeros_like(wide3)
    span = (ROWS1 + 2) * 8
    for dx in range(3):
        for dy in range(3):
            w1 = inlet_two[dy, dx].astype(F32)[:, :16]
            w2 = middle_two[dy, dx].astype(F32)
            for i in range(ROWS1):
                for half in range(2):
                    at = (3 * half + dx) * span + (i + dy) * 8
                    wide1[32 * i : 32 * i + 32, at : at + 8] = w1[:, 8 * half : 8 * half + 8]
            for i in range(ROWS2):
                at = dx * 256 + (i + dy) * 32
                wide2[32 * i : 32 * i + 32, at : at + 32] = w2
    columns = lax.broadcasted_iota(jnp.int32, (ROWS3, 32 * (ROWS3 + 2)), 1)
    offset = columns // 32 - lax.broadcasted_iota(jnp.int32, columns.shape, 0)
    for dx in range(3):
        for o in range(8):
            value = jnp.zeros(columns.shape, F32)
            for dy in range(3):
                line = outlet_two[dy, dx].astype(F32)[o : o + 1]
                line = jnp.concatenate([line] * (ROWS3 + 2), axis=1)
                value = jnp.where(offset == dy, line, value)
            row = (dx * 8 + o) * ROWS3
            wide3[row : row + ROWS3, :] = value
    mid_two[...] = wide2[...].astype(BF)
    last_two[...] = wide3[...].astype(BF)
    lane = lax.broadcasted_iota(jnp.int32, (32, LANES), 1)

    def spread(column):
        return jnp.broadcast_to(column, (32, LANES))

    def split(value):
        high = value.astype(BF).astype(F32)
        return high, (value - high).astype(BF).astype(F32)

    taps = [[spread(inlet_two[dy, dx].astype(F32)[:, 16:17]) for dx in range(3)] for dy in range(3)]
    centre_high, centre_low = split(taps[1][1] + spread(land_bias[...]))
    taps[1][1] = centre_high
    bias_high, bias_low = split(spread(bias_two))
    starts = starts_of(band + 4, ROWS1)
    for b, s in enumerate(starts):
        for i in range(ROWS1):
            value = jnp.where(lane == 48, bias_high, 0.0)
            value = jnp.where(lane == 49, bias_low, value)
            for dx in range(3):
                for dy in range(3):
                    value = jnp.where(lane == dx * 32 + ground_row(band, s + i + dy), taps[dy][dx], value)
            value = jnp.where(lane == 96 + ground_row(band, s + i + 1), centre_low, value)
            first_two[b, 32 * i : 32 * i + 32, 0:LANES] = value.astype(BF)
        first_two[b, :, LANES:] = wide1[...].astype(BF)


def coarse_kernel(
    tile_rows, cols, dests, place, steps, own, west, east, state, first_one, mid_one, last_one,
    bias, scale, coarse_next, noise_one, sends, turned, hidden, active, summed, taps,
):
    px = cols + 2 * EDGE
    rows_before, rows_total, cols_before, cols_total = (place[k] for k in range(4))
    keep, blend = plan(steps[0], (8, cols))
    ext = tile_rows + 10
    pairs = (tile_rows + 8) // 2
    column = cols_before - EDGE + lax.broadcasted_iota(jnp.int32, (px, 256), 0)
    half = lax.broadcasted_iota(jnp.int32, (px, 256), 1) // 128
    inside = jnp.where((column >= 0) & (column < cols_total), 1.0, 0.0)

    windows = [min(14 * k, ext - 16) for k in range(-(-pairs // 7))]
    for k, at in enumerate(windows):
        parts = [
            ref[at : at + 16].reshape(256, cols).astype(F32).T for ref in (west, own, east)
        ]
        whole = jnp.concatenate([parts[0][cols - EDGE :], parts[1], parts[2][:EDGE]], axis=0)
        row = rows_before - 5 + at + lax.broadcasted_iota(jnp.int32, (px, 256), 1) // 16
        whole = jnp.where((row >= 0) & (row < rows_total) & (inside > 0), whole, 0.0)
        turned[k, 0] = pltpu.roll(whole, 1, 0).astype(BF)
        turned[k, 1] = whole.astype(BF)
        turned[k, 2] = pltpu.roll(whole, px - 1, 0).astype(BF)

    def mask(first_row):
        row = rows_before - 5 + first_row + half
        return jnp.where((row >= 0) & (row < rows_total), inside, 0.0)

    for p in range(pairs):
        k = p // 7
        off = 192 - (2 * p - windows[k]) * 16
        acc = jnp.dot(turned[k, 0], first_one[0, off : off + 256], preferred_element_type=F32)
        for dx in (1, 2):
            acc += jnp.dot(turned[k, dx], first_one[dx, off : off + 256], preferred_element_type=F32)
        low = silu(acc + bias[0:1, :]).astype(BF)
        hidden[p] = low
        value = low.astype(F32)
        square = value * value
        scaled = []
        for h in range(2):
            mean = jnp.mean(square[:, h * 128 : (h + 1) * 128], axis=1, keepdims=True)
            scaled.append(value[:, h * 128 : (h + 1) * 128] * lax.rsqrt(mean + 1e-06))
        act = silu(jnp.concatenate(scaled, axis=1) * scale[...]) * mask(1 + 2 * p)
        active[p, :, 0:256] = pltpu.roll(act, 1, 0).astype(BF)
        active[p, :, 256:512] = act.astype(BF)
        active[p, :, 512:768] = pltpu.roll(act, px - 1, 0).astype(BF)

    for p in range(pairs - 1):
        acc = None
        for dx in range(3):
            for q in range(2):
                at = dx * 512 + q * 256
                term = jnp.dot(
                    active[p + q, :, dx * 256 : (dx + 1) * 256], mid_one[at : at + 256],
                    preferred_element_type=F32,
                )
                acc = term if acc is None else acc + term
        rest = jnp.concatenate([hidden[p, :, 128:256], hidden[p + 1, :, 0:128]], axis=1)
        summed[p] = ((acc + rest.astype(F32)) * mask(2 + 2 * p)).astype(BF)

    for p in range(pairs - 1):
        taps[p] = lax.dot_general(
            last_one[...], summed[p], (((1,), (1,)), ((), ())), preferred_element_type=F32
        )
    each = tile_rows // dests
    for p in range(pairs - 2):
        noise = None
        for dx in range(3):
            at = EDGE - 1 + dx
            term = (
                taps[p, dx * 32 : dx * 32 + 16, at : at + cols]
                + taps[p + 1, dx * 32 + 16 : dx * 32 + 32, at : at + cols]
            )
            noise = term if noise is None else noise + term
        made = []
        for i in range(2):
            y = 2 * p - 2 + i
            part = noise[8 * i : 8 * i + 8]
            if 0 <= y < tile_rows:
                rows = pl.ds(y, 8, stride=tile_rows)
                after = keep * state[rows, :] + blend * part
                noise_one[rows, :] = part
                coarse_next[rows, :] = after
            else:
                after = keep * own[y + 5].astype(F32)[0:8] + blend * part
            made.append(after)
        made = jnp.concatenate(made, axis=0).astype(BF)
        for d in range(dests):
            slot = 2 * p - each * d
            if 0 <= slot < each + 4:
                sends[d, slot * 8 : slot * 8 + 16, :] = made


def fine_kernel(
    band, quarter, place, steps, coarse, fine_far, own, land, above, below, back, first_two, mid_two, last_two,
    fine_far_next, noise_far, rows_of, states, lifted, ground, hidden, summed, fine, fine_next, noise_two, sems,
):
    bring = pltpu.make_async_copy(fine_far, fine, sems.at[0])
    bring.start()
    keep, blend = plan(steps[1], (8, LANES))
    keep, blend = (jnp.concatenate([v] * 4, axis=1) for v in (keep, blend))
    top = jnp.where(place[4] > 0, 1.0, 0.0)
    bottom = jnp.where(place[4] < place[5] - 1, 1.0, 0.0)
    ext = band + 6
    quota = band // 4
    sources = quarter // LANES
    tall = ext * 8

    def edge(value, by):
        lane = lax.broadcasted_iota(jnp.int32, value.shape, 1)
        if by > 0:
            return jnp.where(lane == 0, 0.0, pltpu.roll(value, 1, 1))
        return jnp.where(lane == quarter - 1, 0.0, pltpu.roll(value, quarter - 1, 1))

    def keep_phase(ref, j, rows, value):
        ref[j + 1, rows, :] = value.astype(BF)
        if j == 0:
            ref[5, rows, :] = edge(value, -1).astype(BF)
        if j == 3:
            ref[0, rows, :] = edge(value, 1).astype(BF)

    field = lax.broadcasted_iota(jnp.int32, (16, quarter), 0)
    for j in range(4):
        upper = above[j].astype(F32) * top
        lower = below[j].astype(F32) * bottom
        mine = own[j].astype(F32)
        high = jnp.where(field < 8, upper[16:32], mine[0:16])
        low = jnp.where(field < 8, mine[tall - 48 :], lower[0:16])
        keep_phase(
            states, j, slice(0, tall),
            jnp.concatenate([upper[0:16], high, mine[16 : tall - 48], low, lower[16:32]], axis=0),
        )
        tail = jnp.concatenate([upper[24:32], lower[0:8]], axis=0)
        tail = jnp.where(field < 2, 1.0, tail)
        keep_phase(
            ground, j, slice(0, 32), jnp.concatenate([land[j].astype(F32), tail], axis=0)
        )

    for m in range(sources):
        block = coarse[m].astype(F32)
        rows = [block[8 * j : 8 * j + 8] for j in range(quota + 4)]
        rows[1] = top * rows[1] + (1.0 - top) * rows[2]
        rows[quota + 2] = bottom * rows[quota + 2] + (1.0 - bottom) * rows[quota + 1]
        for e in range(ext):
            k, phase = divmod(e - 3, 4)
            j = k + 2
            other, near, far = (
                (j - 1, 0.625, 0.375), (j - 1, 0.875, 0.125), (j + 1, 0.875, 0.125), (j + 1, 0.625, 0.375),
            )[phase]
            value = near * rows[j] + far * rows[other]
            if e < 3:
                value = value * top
            if e >= band + 3:
                value = value * bottom
            rows_of[8 * e : 8 * e + 8, m * LANES : (m + 1) * LANES] = value
    centre = rows_of[...]
    lane = lax.broadcasted_iota(jnp.int32, centre.shape, 1)
    before = jnp.where(lane == 0, centre, pltpu.roll(centre, 1, 1))
    after = jnp.where(lane == quarter - 1, centre, pltpu.roll(centre, quarter - 1, 1))
    for j, (side, near, far) in enumerate(
        ((before, 0.625, 0.375), (before, 0.875, 0.125), (after, 0.875, 0.125), (after, 0.625, 0.375))
    ):
        keep_phase(lifted, j, slice(0, tall), near * centre + far * side)

    done = 0
    for b, s in enumerate(starts_of(band + 4, ROWS1)):
        for j in range(4):
            window = slice(8 * s, 8 * (s + ROWS1 + 2))
            operand = [ground[j], ground[j + 1], ground[j + 2], ground[j + 1]]
            operand += [states[j + k, window] for k in range(3)]
            operand += [lifted[j + k, window] for k in range(3)]
            value = jnp.dot(
                first_two[b], jnp.concatenate(operand, axis=0), preferred_element_type=F32
            )[32 * (done - s) :]
            value = silu(value)
            parts = []
            for i in range(done, s + ROWS1):
                part = value[32 * (i - done) : 32 * (i - done) + 32]
                if i < 2:
                    part = part * top
                if i >= band + 2:
                    part = part * bottom
                parts.append(part)
            keep_phase(hidden, j, slice(32 * done, 32 * (s + ROWS1)), jnp.concatenate(parts, axis=0))
        done = s + ROWS1

    done = 0
    for s in starts_of(band + 2, ROWS2):
        for j in range(4):
            window = slice(32 * s, 32 * (s + ROWS2 + 2))
            value = jnp.dot(
                mid_two[...], jnp.concatenate([hidden[j + k, window] for k in range(3)], axis=0),
                preferred_element_type=F32,
            )
            for i in range(done, s + ROWS2):
                rows = slice(32 * (i + 1), 32 * (i + 2))
                part = value[32 * (i - s) : 32 * (i - s) + 32] + hidden[j + 1, rows].astype(F32)
                if i < 1:
                    part = part * top
                if i >= band + 1:
                    part = part * bottom
                summed[j, 32 * i : 32 * i + 32] = part.astype(BF)
        done = s + ROWS2

    high = 8 * ROWS3
    bring.wait()
    sends = []
    for s in range(0, band, ROWS3):
        made = [
            jnp.dot(last_two[...], summed[j, 32 * s : 32 * (s + ROWS3 + 2)], preferred_element_type=F32)
            for j in range(4)
        ]
        west = [edge(made[3][0:high], 1)] + [made[j][0:high] for j in range(3)]
        east = [made[j][2 * high :] for j in range(1, 4)] + [edge(made[0][2 * high :], -1)]
        phases = [west[j] + made[j][high : 2 * high] + east[j] for j in range(4)]
        for m in range(sources):
            value = jnp.concatenate([p[:, m * LANES : (m + 1) * LANES] for p in phases], axis=1)
            rough = value.astype(BF)
            fine_part = (value - rough.astype(F32)).astype(BF)
            noise = jnp.dot(
                jnp.concatenate([rough, fine_part], axis=0), back[...], preferred_element_type=F32
            )
            noise = noise[0:high] + noise[high:]
            cols = slice(4 * LANES * m, 4 * LANES * (m + 1))
            for o in range(8):
                rows = slice(s, s + ROWS3)
                part = noise[ROWS3 * o : ROWS3 * o + ROWS3]
                noise_two[o, rows, cols] = part
                fine_next[o, rows, cols] = keep * fine[o, rows, cols] + blend * part
        rows = pl.ds(s, ROWS3)
        for k, (near, far) in enumerate(((noise_two, noise_far), (fine_next, fine_far_next))):
            sem = sems.at[1 + 2 * (s // ROWS3) + k]
            sends.append(pltpu.make_async_copy(near.at[:, rows], far.at[:, rows], sem))
            sends[-1].start()
    for send in sends:
        send.wait()


def turn_matrix():
    made = np.zeros((4 * LANES, 4 * LANES))
    for n in range(4 * LANES):
        made[n, (n % 4) * LANES + n // 4] = 1
    return made


def order_matrix(band):
    made = np.zeros((80 + 8 * (band + 2), 9 * band))
    for o in range(8):
        for y in range(3):
            made[8 * y + o, o * band + band - 3 + y] = 1
            made[32 + 8 * (y + 1) + o, o * band + y] = 1
        for y in range(band):
            made[80 + 8 * (y + 1) + o, o * band + y] = 1
    for y in range(8):
        made[24 + y, 8 * band + band - 8 + y] = 1
        made[32 + y, 8 * band + y] = 1
    for y in range(band):
        made[64 + y, 8 * band + y] = 1
    return made


def body(
    step_index, coarse_state, coarse_forcing, fine_state, land_mask, inlet_one, timing_one, scale_one,
    middle_one, outlet_one, inlet_two, timing_two, land_bias, middle_two, outlet_two,
):
    fields, tile_rows, cols = coarse_state.shape
    _, band, width = fine_state.shape
    row_count, col_count = lax.axis_size("row"), lax.axis_size("col")
    row_at, col_at = lax.axis_index("row"), lax.axis_index("col")
    count = row_count * col_count
    state = coarse_state.reshape(fields * tile_rows, cols)
    forcing = coarse_forcing.reshape(fields * tile_rows, cols)
    fine = fine_state.reshape(fields * band, width)
    quarter = width // 4
    place = jnp.stack(
        [
            row_at * tile_rows, jnp.int32(row_count * tile_rows), col_at * cols,
            jnp.int32(col_count * cols), row_at * col_count + col_at, jnp.int32(count),
        ]
    ).astype(jnp.int32)
    ladder = ladder_rows(timing_one.shape[0])

    comb, first_rows, last_rows = pl.pallas_call(
        functools.partial(pack_kernel, tile_rows),
        out_shape=(
            jax.ShapeDtypeStruct((tile_rows, 2 * fields, cols), BF),
            jax.ShapeDtypeStruct((5, 2 * fields, cols), BF),
            jax.ShapeDtypeStruct((5, 2 * fields, cols), BF),
        ),
        in_specs=[ANY] * 2,
        out_specs=[VMEM] * 3,
        scratch_shapes=[
            pltpu.VMEM((fields * tile_rows, cols), F32),
            pltpu.VMEM((fields * tile_rows, cols), F32),
            pltpu.VMEM((fields * tile_rows, cols), BF),
            pltpu.SemaphoreType.DMA((2,)),
        ],
        compiler_params=params(8),
        name="pack",
    )(state, forcing)
    north = lax.ppermute(last_rows, "row", shift_pairs(row_count, 1))
    south = lax.ppermute(first_rows, "row", shift_pairs(row_count, -1))

    turn = turn_matrix()
    split = 1024
    part = split // 4
    shapes = (8 * (band + 2), 16, 32, 32)
    own, ground, to_next, to_prev = pl.pallas_call(
        sort_kernel,
        grid=(width // split,),
        out_shape=[jax.ShapeDtypeStruct((4, rows, quarter), BF) for rows in shapes],
        in_specs=[
            pl.BlockSpec((fields * band, split), lambda n: (0, n)),
            pl.BlockSpec((band, split), lambda n: (0, n)),
            pl.BlockSpec((4 * LANES, 4 * LANES), lambda n: (0, 0)),
            pl.BlockSpec((80 + 8 * (band + 2), 9 * band), lambda n: (0, 0)),
        ],
        out_specs=[pl.BlockSpec((4, rows, part), lambda n: (0, 0, n)) for rows in shapes],
        compiler_params=params(24),
        name="sort",
    )(fine, land_mask, jnp.asarray(turn, BF), jnp.asarray(order_matrix(band), BF))
    above = lax.ppermute(to_next, ("row", "col"), shift_pairs(count, 1))
    below = lax.ppermute(to_prev, ("row", "col"), shift_pairs(count, -1))

    tall = jnp.concatenate([north, comb, south], axis=0)
    west = lax.ppermute(tall, "col", shift_pairs(col_count, 1))
    east = lax.ppermute(tall, "col", shift_pairs(col_count, -1))

    first_one, mid_one, last_one, bias = pl.pallas_call(
        coarse_weights,
        out_shape=(
            jax.ShapeDtypeStruct((3, 448, 256), BF),
            jax.ShapeDtypeStruct((1536, 256), BF),
            jax.ShapeDtypeStruct((96, 256), BF),
            jax.ShapeDtypeStruct((8, 256), F32),
        ),
        in_specs=[SMEM] + [WHOLE] * 5,
        out_specs=[VMEM] * 4,
        compiler_params=params(8),
        name="coarse_weights",
    )(step_index, ladder, timing_one, inlet_one, middle_one, outlet_one)
    blocks = len(starts_of(band + 4, ROWS1))
    deep = LANES + 6 * 8 * (ROWS1 + 2)
    first_two, mid_two, last_two = pl.pallas_call(
        functools.partial(fine_weights, band),
        out_shape=(
            jax.ShapeDtypeStruct((blocks, 32 * ROWS1, deep), BF),
            jax.ShapeDtypeStruct((32 * ROWS2, 768), BF),
            jax.ShapeDtypeStruct((24 * ROWS3, 32 * (ROWS3 + 2)), BF),
        ),
        in_specs=[SMEM] + [WHOLE] * 6,
        out_specs=[VMEM] * 3,
        scratch_shapes=[
            pltpu.VMEM((32 * ROWS1, deep - LANES), F32),
            pltpu.VMEM((32 * ROWS2, 768), F32),
            pltpu.VMEM((24 * ROWS3, 32 * (ROWS3 + 2)), F32),
        ],
        compiler_params=params(8),
        name="fine_weights",
    )(step_index, ladder, timing_two, inlet_two, middle_two, outlet_two, land_bias[:, None])

    px = cols + 2 * EDGE
    pairs = (tile_rows + 8) // 2
    each = tile_rows // col_count
    coarse_next, noise_one, sends = pl.pallas_call(
        functools.partial(coarse_kernel, tile_rows, cols, col_count),
        out_shape=(
            jax.ShapeDtypeStruct((fields * tile_rows, cols), F32),
            jax.ShapeDtypeStruct((fields * tile_rows, cols), F32),
            jax.ShapeDtypeStruct((col_count, (each + 4) * fields, cols), BF),
        ),
        in_specs=[SMEM] * 2 + [VMEM] * 9,
        out_specs=[VMEM] * 3,
        scratch_shapes=[
            pltpu.VMEM((-(-pairs // 7), 3, px, 256), BF),
            pltpu.VMEM((pairs, px, 256), BF),
            pltpu.VMEM((pairs, px, 768), BF),
            pltpu.VMEM((pairs - 1, px, 256), BF),
            pltpu.VMEM((pairs - 1, 96, px), F32),
        ],
        compiler_params=params(40),
        name="coarse",
    )(
        place, step_index, tall, west, east, state, first_one, mid_one, last_one, bias,
        jnp.tile(scale_one, 2)[None, :],
    )

    arrived = lax.all_to_all(sends, "col", split_axis=0, concat_axis=0, tiled=True)

    fine_next, noise_two = pl.pallas_call(
        functools.partial(fine_kernel, band, quarter),
        out_shape=(
            jax.ShapeDtypeStruct((fields, band, width), F32),
            jax.ShapeDtypeStruct((fields, band, width), F32),
        ),
        in_specs=[SMEM] * 2 + [VMEM, ANY] + [VMEM] * 8,
        out_specs=[ANY] * 2,
        scratch_shapes=[
            pltpu.VMEM(((band + 6) * 8, quarter), F32),
            pltpu.VMEM((6, (band + 6) * 8, quarter), BF),
            pltpu.VMEM((6, (band + 6) * 8, quarter), BF),
            pltpu.VMEM((6, 32, quarter), BF),
            pltpu.VMEM((6, (band + 4) * 32, quarter), BF),
            pltpu.VMEM((4, (band + 2) * 32, quarter), BF),
            pltpu.VMEM((fields, band, width), F32),
            pltpu.VMEM((fields, band, width), F32),
            pltpu.VMEM((fields, band, width), F32),
            pltpu.SemaphoreType.DMA((1 + 2 * (band // ROWS3),)),
        ],
        compiler_params=params(56),
        name="fine",
    )(
        place, step_index, arrived, fine_state, own, ground, above, below, jnp.asarray(turn.T, BF),
        first_two, mid_two, last_two,
    )

    return (
        coarse_next.reshape(coarse_state.shape),
        noise_one.reshape(coarse_state.shape),
        fine_next,
        noise_two,
    )


def solution(mesh):
    return jax.shard_map(
        body,
        mesh=mesh,
        in_specs=(
            P(), P(None, "row", "col"), P(None, "row", "col"), P(None, ("row", "col"), None),
            P(("row", "col"), None), P(), P(), P(), P(), P(), P(), P(), P(), P(), P(),
        ),
        out_specs=(
            P(None, "row", "col"), P(None, "row", "col"), P(None, ("row", "col"), None),
            P(None, ("row", "col"), None),
        ),
        check_vma=False,
    )
```

```python
import functools
import math

import jax
import jax.numpy as jnp
import numpy as np
from jax import lax
from jax.experimental import pallas as pl
from jax.experimental.pallas import tpu as pltpu
from jax.sharding import PartitionSpec as P

BF = jnp.bfloat16
F32 = jnp.float32
VMEM = pl.BlockSpec(memory_space=pltpu.VMEM)
SMEM = pl.BlockSpec(memory_space=pltpu.SMEM)
ANY = pl.BlockSpec(memory_space=pl.ANY)
WHOLE = pl.BlockSpec()
EDGE = 16
ROWS1 = 6
ROWS2 = 6
ROWS3 = 8
LANES = 128


def params(mib):
    return pltpu.CompilerParams(vmem_limit_bytes=mib << 20)


def silu(v):
    return v * (0.5 * jnp.tanh(0.5 * v) + 0.5)


def starts_of(rows, height):
    return [min(s, rows - height) for s in range(0, rows, height)]


def shift_pairs(count, by):
    return [(i, (i + by) % count) for i in range(count)]


def alpha_bar(moment):
    return jnp.cos((moment / 1000.0 + 0.008) / 1.008 * (math.pi / 2.0)) ** 2


def plan(step, shape):
    current_time = jnp.full(shape, step.astype(F32), F32)
    current = alpha_bar(current_time)
    earlier = alpha_bar(current_time - 50.0)
    keeping = jnp.sqrt(earlier / current)
    blending = jnp.sqrt(1.0 - earlier) - jnp.sqrt(earlier) * jnp.sqrt(1.0 - current) / jnp.sqrt(
        current
    )
    return (keeping, blending)


def embed(step, ladder, timing):
    half = ladder.shape[1] // 2
    angles = step.astype(F32) * ladder[...]
    lane = lax.broadcasted_iota(jnp.int32, angles.shape, 1)
    feature = jnp.where(lane < half, jnp.sin(angles), jnp.cos(angles))
    parts = []
    for _ in range(3):
        part = feature.astype(BF)
        feature = feature - part.astype(F32)
        parts.append(part)
    return sum(jnp.dot(part, timing, preferred_element_type=F32) for part in parts)


def ladder_rows(width):
    steps = np.exp(-math.log(10000.0) * np.arange(width // 2) / (width // 2))
    return jnp.asarray(np.tile(np.concatenate([steps, steps]), (8, 1)), F32)


def pack_kernel(tile_rows, state, forcing, comb, top, bottom, near, wide, narrow, sems):
    copies = [
        pltpu.make_async_copy(state, near, sems.at[0]),
        pltpu.make_async_copy(forcing, narrow, sems.at[1]),
    ]
    for copy in copies:
        copy.start()
    for copy in copies:
        copy.wait()
    wide[...] = narrow[...].astype(F32)
    for y in range(tile_rows):
        made = jnp.concatenate(
            [near[pl.ds(y, 8, stride=tile_rows), :], wide[pl.ds(y, 8, stride=tile_rows), :]], axis=0
        ).astype(BF)
        comb[y] = made
        if y < 5:
            top[y] = made
        if y >= tile_rows - 5:
            bottom[y - tile_rows + 5] = made


def edge_kernel(tile_rows, north, comb, south, tile, first_cols, last_cols):
    cols = comb.shape[2]

    def row(e):
        if e < 5:
            return north[e]
        return comb[e - 5] if e < tile_rows + 5 else south[min(e - tile_rows - 5, 4)]

    for g in range(tile.shape[1] // LANES):
        block = jnp.concatenate([row(6 * g + i).astype(F32) for i in range(8)], axis=0)
        turned = block.T.astype(BF)
        at = slice(g * LANES, (g + 1) * LANES)
        tile[:, at] = turned
        first_cols[:, at] = turned[0:EDGE]
        last_cols[:, at] = turned[cols - EDGE :]


def sort_kernel(fine, land, turn, order, own, ground, to_next, to_prev):
    blocks = []
    for m in range(fine.shape[1] // (4 * LANES)):
        cols = slice(4 * LANES * m, 4 * LANES * (m + 1))
        blocks += [fine[:, cols], land[:, cols].astype(F32)]
    high = fine.shape[0] + land.shape[0]
    sorted_all = jnp.dot(
        jnp.concatenate(blocks, axis=0).astype(BF), turn[...], preferred_element_type=F32
    )
    for m in range(fine.shape[1] // (4 * LANES)):
        block = sorted_all[m * high : (m + 1) * high].astype(BF)
        made = jnp.dot(order[...], block, preferred_element_type=F32).astype(BF)
        at = slice(m * LANES, (m + 1) * LANES)
        for j in range(4):
            part = made[:, j * LANES : (j + 1) * LANES]
            to_next[j, :, at] = part[0:32]
            to_prev[j, :, at] = part[32:64]
            ground[j, :, at] = part[64:80]
            own[j, :, at] = part[80:]


def ground_row(band, e):
    if e < 3:
        return 21 + e
    return e - 3 if e < band + 3 else 24 + e - band - 3


def coarse_weights(
    steps, ladder, timing, inlet_one, middle_one, outlet_one, first_one, mid_one, last_one, bias,
):
    made = embed(steps[0], ladder, timing[...])
    bias[...] = jnp.concatenate([made, made], axis=1)
    first_one[...] = jnp.zeros_like(first_one)
    for t in range(3):
        for dx in range(3):
            for i in range(2):
                for dy in range(3):
                    at = dx * LANES + (2 * t + i + dy) * 16
                    first_one[t, at : at + 16, i * 128 : (i + 1) * 128] = inlet_one[dy, dx]
    mid_one[...] = jnp.zeros_like(mid_one)
    last_one[...] = jnp.zeros_like(last_one)
    for dx in range(3):
        for dy in range(3):
            turned = middle_one[dy, dx].astype(F32).T.astype(BF)
            for i in range(2):
                at = dx * 512 + (i + dy) * 128
                mid_one[at : at + 128, i * 128 : (i + 1) * 128] = turned
    for dx in range(3):
        for slot in range(2):
            pieces = []
            for i in range(2):
                halves = []
                for par in range(2):
                    dy = 2 * slot + par - i
                    halves.append(
                        outlet_one[dy, dx].astype(F32) if 0 <= dy <= 2 else jnp.zeros((8, 128), F32)
                    )
                pieces.append(jnp.concatenate(halves, axis=1))
            at = dx * 32 + slot * 16
            last_one[at : at + 16, :] = jnp.concatenate(pieces, axis=0).astype(BF)


def fine_weights(
    band, steps, ladder, timing, inlet_two, middle_two, outlet_two, land_bias, first_two, mid_two, last_two,
    wide1, wide2, wide3,
):
    bias_two = embed(steps[1], ladder, timing[...])[0:1].T
    wide1[...] = jnp.zeros_like(wide1)
    wide2[...] = jnp.zeros_like(wide2)
    wide3[...] = jnp.zeros_like(wide3)
    span = (ROWS1 + 2) * 8
    for dx in range(3):
        for dy in range(3):
            w1 = inlet_two[dy, dx].astype(F32)[:, :16]
            w2 = middle_two[dy, dx].astype(F32)
            for i in range(ROWS1):
                for half in range(2):
                    at = (3 * half + dx) * span + (i + dy) * 8
                    wide1[32 * i : 32 * i + 32, at : at + 8] = w1[:, 8 * half : 8 * half + 8]
            for i in range(ROWS2):
                at = dx * 256 + (i + dy) * 32
                wide2[32 * i : 32 * i + 32, at : at + 32] = w2
    columns = lax.broadcasted_iota(jnp.int32, (ROWS3, 32 * (ROWS3 + 2)), 1)
    offset = columns // 32 - lax.broadcasted_iota(jnp.int32, columns.shape, 0)
    for dx in range(3):
        for o in range(8):
            value = jnp.zeros(columns.shape, F32)
            for dy in range(3):
                line = outlet_two[dy, dx].astype(F32)[o : o + 1]
                line = jnp.concatenate([line] * (ROWS3 + 2), axis=1)
                value = jnp.where(offset == dy, line, value)
            row = (dx * 8 + o) * ROWS3
            wide3[row : row + ROWS3, :] = value
    mid_two[...] = wide2[...].astype(BF)
    last_two[...] = wide3[...].astype(BF)
    lane = lax.broadcasted_iota(jnp.int32, (32, LANES), 1)

    def spread(column):
        return jnp.broadcast_to(column, (32, LANES))

    def split(value):
        high = value.astype(BF).astype(F32)
        return high, (value - high).astype(BF).astype(F32)

    taps = [[spread(inlet_two[dy, dx].astype(F32)[:, 16:17]) for dx in range(3)] for dy in range(3)]
    centre_high, centre_low = split(taps[1][1] + spread(land_bias[...]))
    taps[1][1] = centre_high
    bias_high, bias_low = split(spread(bias_two))
    starts = starts_of(band + 4, ROWS1)
    for b, s in enumerate(starts):
        for i in range(ROWS1):
            value = jnp.where(lane == 48, bias_high, 0.0)
            value = jnp.where(lane == 49, bias_low, value)
            for dx in range(3):
                for dy in range(3):
                    value = jnp.where(lane == dx * 32 + ground_row(band, s + i + dy), taps[dy][dx], value)
            value = jnp.where(lane == 96 + ground_row(band, s + i + 1), centre_low, value)
            first_two[b, 32 * i : 32 * i + 32, 0:LANES] = value.astype(BF)
        first_two[b, :, LANES:] = wide1[...].astype(BF)


def coarse_kernel(
    tile_rows, cols, dests, steps, north, south, own, west, east, state, first_one, mid_one, last_one,
    bias, scale, coarse_next, noise_one, sends, turned, hidden, active, summed, taps,
):
    px = cols + 2 * EDGE
    rows_before, cols_before = lax.axis_index("row") * tile_rows, lax.axis_index("col") * cols
    rows_total, cols_total = lax.axis_size("row") * tile_rows, lax.axis_size("col") * cols
    keep, blend = plan(steps[0], (8, cols))
    ext = tile_rows + 10
    pairs = (tile_rows + 8) // 2
    column = cols_before - EDGE + lax.broadcasted_iota(jnp.int32, (px, 256), 0)
    half = lax.broadcasted_iota(jnp.int32, (px, 256), 1) // 128
    inside = jnp.where((column >= 0) & (column < cols_total), 1.0, 0.0)

    gains = jnp.concatenate([scale[...], scale[...]], axis=1)
    for g in range(-(-pairs // 3)):
        lanes = slice(g * LANES, (g + 1) * LANES)
        whole = jnp.concatenate([west[:, lanes], own[:, lanes], east[:, lanes]], axis=0).astype(F32)
        row = rows_before - 5 + 6 * g + lax.broadcasted_iota(jnp.int32, (px, LANES), 1) // 16
        whole = jnp.where((row >= 0) & (row < rows_total) & (inside[:, 0:LANES] > 0), whole, 0.0)
        turned[g, :, 0:LANES] = pltpu.roll(whole, 1, 0).astype(BF)
        turned[g, :, LANES : 2 * LANES] = whole.astype(BF)
        turned[g, :, 2 * LANES :] = pltpu.roll(whole, px - 1, 0).astype(BF)

    def mask(first_row):
        row = rows_before - 5 + first_row + half
        return jnp.where((row >= 0) & (row < rows_total), inside, 0.0)

    for p in range(pairs):
        acc = jnp.dot(turned[p // 3], first_one[p % 3], preferred_element_type=F32)
        low = silu(acc + bias[0:1, :]).astype(BF)
        hidden[p] = low
        value = low.astype(F32)
        square = value * value
        scaled = []
        for h in range(2):
            mean = jnp.mean(square[:, h * 128 : (h + 1) * 128], axis=1, keepdims=True)
            scaled.append(value[:, h * 128 : (h + 1) * 128] * lax.rsqrt(mean + 1e-06))
        act = silu(jnp.concatenate(scaled, axis=1) * gains) * mask(1 + 2 * p)
        active[p, :, 0:256] = pltpu.roll(act, 1, 0).astype(BF)
        active[p, :, 256:512] = act.astype(BF)
        active[p, :, 512:768] = pltpu.roll(act, px - 1, 0).astype(BF)

    for p in range(0, pairs - 1, 2):
        size = min(2, pairs - 1 - p)
        parts = [
            active[p + q : p + q + size, :, dx * 256 : (dx + 1) * 256].reshape(size * px, 256)
            for dx in range(3)
            for q in range(2)
        ]
        acc = jnp.dot(jnp.concatenate(parts, axis=1), mid_one[...], preferred_element_type=F32)
        for k in range(size):
            n = p + k
            rest = jnp.concatenate([hidden[n, :, 128:256], hidden[n + 1, :, 0:128]], axis=1)
            value = acc[k * px : (k + 1) * px] + rest.astype(F32)
            summed[n] = (value * mask(2 + 2 * n)).astype(BF)

    for p in range(pairs - 1):
        taps[p] = lax.dot_general(
            last_one[...], summed[p], (((1,), (1,)), ((), ())), preferred_element_type=F32
        )
    each = tile_rows // dests
    for p in range(pairs - 2):
        noise = None
        for dx in range(3):
            at = EDGE - 1 + dx
            term = (
                taps[p, dx * 32 : dx * 32 + 16, at : at + cols]
                + taps[p + 1, dx * 32 + 16 : dx * 32 + 32, at : at + cols]
            )
            noise = term if noise is None else noise + term
        made = []
        for i in range(2):
            y = 2 * p - 2 + i
            part = noise[8 * i : 8 * i + 8]
            if 0 <= y < tile_rows:
                rows = pl.ds(y, 8, stride=tile_rows)
                after = keep * state[rows, :] + blend * part
                noise_one[rows, :] = part
                coarse_next[rows, :] = after
            else:
                edge = north[y + 5] if y < 0 else south[y - tile_rows]
                after = keep * edge.astype(F32)[0:8] + blend * part
            made.append(after)
        made = jnp.concatenate(made, axis=0).astype(BF)
        for d in range(dests):
            slot = 2 * p - each * d
            if 0 <= slot < each + 4:
                sends[d, slot * 8 : slot * 8 + 16, :] = made


def fine_kernel(
    band, quarter, steps, coarse, fine_far, own, land, above, below, back, first_two, mid_two, last_two,
    fine_far_next, noise_far, rows_of, states, lifted, ground, hidden, summed, fine, fine_next, noise_two, sems,
):
    bring = pltpu.make_async_copy(fine_far, fine, sems.at[0])
    bring.start()
    keep, blend = plan(steps[1], (8, LANES))
    keep, blend = (jnp.concatenate([v] * 4, axis=1) for v in (keep, blend))
    position = lax.axis_index("row") * lax.axis_size("col") + lax.axis_index("col")
    count = lax.axis_size("row") * lax.axis_size("col")
    top = jnp.where(position > 0, 1.0, 0.0)
    bottom = jnp.where(position < count - 1, 1.0, 0.0)
    ext = band + 6
    quota = band // 4
    sources = quarter // LANES
    tall = ext * 8

    def edge(value, by):
        lane = lax.broadcasted_iota(jnp.int32, value.shape, 1)
        if by > 0:
            return jnp.where(lane == 0, 0.0, pltpu.roll(value, 1, 1))
        return jnp.where(lane == quarter - 1, 0.0, pltpu.roll(value, quarter - 1, 1))

    def keep_phase(ref, j, rows, value):
        ref[j + 1, rows, :] = value.astype(BF)
        if j == 0:
            ref[5, rows, :] = edge(value, -1).astype(BF)
        if j == 3:
            ref[0, rows, :] = edge(value, 1).astype(BF)

    field = lax.broadcasted_iota(jnp.int32, (16, quarter), 0)
    for j in range(4):
        upper = above[j].astype(F32) * top
        lower = below[j].astype(F32) * bottom
        mine = own[j].astype(F32)
        high = jnp.where(field < 8, upper[16:32], mine[0:16])
        low = jnp.where(field < 8, mine[tall - 48 :], lower[0:16])
        keep_phase(
            states, j, slice(0, tall),
            jnp.concatenate([upper[0:16], high, mine[16 : tall - 48], low, lower[16:32]], axis=0),
        )
        tail = jnp.concatenate([upper[24:32], lower[0:8]], axis=0)
        tail = jnp.where(field < 2, 1.0, tail)
        keep_phase(
            ground, j, slice(0, 32), jnp.concatenate([land[j].astype(F32), tail], axis=0)
        )

    for m in range(sources):
        block = coarse[m].astype(F32)
        rows = [block[8 * j : 8 * j + 8] for j in range(quota + 4)]
        rows[1] = top * rows[1] + (1.0 - top) * rows[2]
        rows[quota + 2] = bottom * rows[quota + 2] + (1.0 - bottom) * rows[quota + 1]
        for e in range(ext):
            k, phase = divmod(e - 3, 4)
            j = k + 2
            other, near, far = (
                (j - 1, 0.625, 0.375), (j - 1, 0.875, 0.125), (j + 1, 0.875, 0.125), (j + 1, 0.625, 0.375),
            )[phase]
            value = near * rows[j] + far * rows[other]
            if e < 3:
                value = value * top
            if e >= band + 3:
                value = value * bottom
            rows_of[8 * e : 8 * e + 8, m * LANES : (m + 1) * LANES] = value
    centre = rows_of[...]
    lane = lax.broadcasted_iota(jnp.int32, centre.shape, 1)
    before = jnp.where(lane == 0, centre, pltpu.roll(centre, 1, 1))
    after = jnp.where(lane == quarter - 1, centre, pltpu.roll(centre, quarter - 1, 1))
    for j, (side, near, far) in enumerate(
        ((before, 0.625, 0.375), (before, 0.875, 0.125), (after, 0.875, 0.125), (after, 0.625, 0.375))
    ):
        keep_phase(lifted, j, slice(0, tall), near * centre + far * side)

    done = 0
    for b, s in enumerate(starts_of(band + 4, ROWS1)):
        for j in range(4):
            window = slice(8 * s, 8 * (s + ROWS1 + 2))
            operand = [ground[j], ground[j + 1], ground[j + 2], ground[j + 1]]
            operand += [states[j + k, window] for k in range(3)]
            operand += [lifted[j + k, window] for k in range(3)]
            value = jnp.dot(
                first_two[b], jnp.concatenate(operand, axis=0), preferred_element_type=F32
            )[32 * (done - s) :]
            value = silu(value)
            parts = []
            for i in range(done, s + ROWS1):
                part = value[32 * (i - done) : 32 * (i - done) + 32]
                if i < 2:
                    part = part * top
                if i >= band + 2:
                    part = part * bottom
                parts.append(part)
            keep_phase(hidden, j, slice(32 * done, 32 * (s + ROWS1)), jnp.concatenate(parts, axis=0))
        done = s + ROWS1

    done = 0
    for s in starts_of(band + 2, ROWS2):
        for j in range(4):
            window = slice(32 * s, 32 * (s + ROWS2 + 2))
            value = jnp.dot(
                mid_two[...], jnp.concatenate([hidden[j + k, window] for k in range(3)], axis=0),
                preferred_element_type=F32,
            )
            for i in range(done, s + ROWS2):
                rows = slice(32 * (i + 1), 32 * (i + 2))
                part = value[32 * (i - s) : 32 * (i - s) + 32] + hidden[j + 1, rows].astype(F32)
                if i < 1:
                    part = part * top
                if i >= band + 1:
                    part = part * bottom
                summed[j, 32 * i : 32 * i + 32] = part.astype(BF)
        done = s + ROWS2

    high = 8 * ROWS3
    bring.wait()
    sends = []
    for s in range(0, band, ROWS3):
        made = [
            jnp.dot(last_two[...], summed[j, 32 * s : 32 * (s + ROWS3 + 2)], preferred_element_type=F32)
            for j in range(4)
        ]
        west = [edge(made[3][0:high], 1)] + [made[j][0:high] for j in range(3)]
        east = [made[j][2 * high :] for j in range(1, 4)] + [edge(made[0][2 * high :], -1)]
        phases = [west[j] + made[j][high : 2 * high] + east[j] for j in range(4)]
        value = jnp.concatenate(
            [
                jnp.concatenate([p[:, m * LANES : (m + 1) * LANES] for p in phases], axis=1)
                for m in range(sources)
            ],
            axis=0,
        )
        back_all = jnp.dot(value.astype(BF), back[...], preferred_element_type=F32)
        for m in range(sources):
            noise = back_all[m * high : (m + 1) * high]
            cols = slice(4 * LANES * m, 4 * LANES * (m + 1))
            for o in range(8):
                rows = slice(s, s + ROWS3)
                part = noise[ROWS3 * o : ROWS3 * o + ROWS3]
                noise_two[o, rows, cols] = part
                fine_next[o, rows, cols] = keep * fine[o, rows, cols] + blend * part
        rows = pl.ds(s, ROWS3)
        for k, (near, far) in enumerate(((noise_two, noise_far), (fine_next, fine_far_next))):
            sem = sems.at[1 + 2 * (s // ROWS3) + k]
            sends.append(pltpu.make_async_copy(near.at[:, rows], far.at[:, rows], sem))
            sends[-1].start()
    for send in sends:
        send.wait()


def turn_matrix():
    made = np.zeros((4 * LANES, 4 * LANES))
    for n in range(4 * LANES):
        made[n, (n % 4) * LANES + n // 4] = 1
    return made


def order_matrix(band):
    made = np.zeros((80 + 8 * (band + 2), 9 * band))
    for o in range(8):
        for y in range(3):
            made[8 * y + o, o * band + band - 3 + y] = 1
            made[32 + 8 * (y + 1) + o, o * band + y] = 1
        for y in range(band):
            made[80 + 8 * (y + 1) + o, o * band + y] = 1
    for y in range(8):
        made[24 + y, 8 * band + band - 8 + y] = 1
        made[32 + y, 8 * band + y] = 1
    for y in range(band):
        made[64 + y, 8 * band + y] = 1
    return made


def body(
    step_index, coarse_state, coarse_forcing, fine_state, land_mask, inlet_one, timing_one, scale_one,
    middle_one, outlet_one, inlet_two, timing_two, land_bias, middle_two, outlet_two,
):
    fields, tile_rows, cols = coarse_state.shape
    _, band, width = fine_state.shape
    row_count, col_count = lax.axis_size("row"), lax.axis_size("col")
    count = row_count * col_count
    state = coarse_state.reshape(fields * tile_rows, cols)
    forcing = coarse_forcing.reshape(fields * tile_rows, cols)
    fine = fine_state.reshape(fields * band, width)
    quarter = width // 4
    ladder = ladder_rows(timing_one.shape[0])

    comb, first_rows, last_rows = pl.pallas_call(
        functools.partial(pack_kernel, tile_rows),
        out_shape=(
            jax.ShapeDtypeStruct((tile_rows, 2 * fields, cols), BF),
            jax.ShapeDtypeStruct((5, 2 * fields, cols), BF),
            jax.ShapeDtypeStruct((5, 2 * fields, cols), BF),
        ),
        in_specs=[ANY] * 2,
        out_specs=[VMEM] * 3,
        scratch_shapes=[
            pltpu.VMEM((fields * tile_rows, cols), F32),
            pltpu.VMEM((fields * tile_rows, cols), F32),
            pltpu.VMEM((fields * tile_rows, cols), BF),
            pltpu.SemaphoreType.DMA((2,)),
        ],
        compiler_params=params(60),
        name="pack",
    )(state, forcing)
    north = lax.ppermute(last_rows, "row", shift_pairs(row_count, 1))
    south = lax.ppermute(first_rows, "row", shift_pairs(row_count, -1))

    turn = turn_matrix()
    split = 2048
    part = split // 4
    shapes = (8 * (band + 2), 16, 32, 32)
    own, ground, to_next, to_prev = pl.pallas_call(
        sort_kernel,
        grid=(width // split,),
        out_shape=[jax.ShapeDtypeStruct((4, rows, quarter), BF) for rows in shapes],
        in_specs=[
            pl.BlockSpec((fields * band, split), lambda n: (0, n)),
            pl.BlockSpec((band, split), lambda n: (0, n)),
            pl.BlockSpec((4 * LANES, 4 * LANES), lambda n: (0, 0)),
            pl.BlockSpec((80 + 8 * (band + 2), 9 * band), lambda n: (0, 0)),
        ],
        out_specs=[pl.BlockSpec((4, rows, part), lambda n: (0, 0, n)) for rows in shapes],
        compiler_params=params(60),
        name="sort",
    )(fine, land_mask, jnp.asarray(turn, BF), jnp.asarray(order_matrix(band), BF))
    north, to_next, to_prev = lax.optimization_barrier((north, to_next, to_prev))
    deep_rows = -(-(tile_rows + 8) // 6) * LANES
    tile, first_cols, last_cols = pl.pallas_call(
        functools.partial(edge_kernel, tile_rows),
        out_shape=(
            jax.ShapeDtypeStruct((cols, deep_rows), BF),
            jax.ShapeDtypeStruct((EDGE, deep_rows), BF),
            jax.ShapeDtypeStruct((EDGE, deep_rows), BF),
        ),
        in_specs=[VMEM] * 3,
        out_specs=[VMEM] * 3,
        compiler_params=params(8),
        name="edges",
    )(north, comb, south)
    west = lax.ppermute(last_cols, "col", shift_pairs(col_count, 1))
    east = lax.ppermute(first_cols, "col", shift_pairs(col_count, -1))
    turned_inlet, first_cols = lax.optimization_barrier(
        (jnp.transpose(inlet_one, (0, 1, 3, 2)), first_cols)
    )
    first_one, mid_one, last_one, bias = pl.pallas_call(
        coarse_weights,
        out_shape=(
            jax.ShapeDtypeStruct((3, 3 * LANES, 256), BF),
            jax.ShapeDtypeStruct((1536, 256), BF),
            jax.ShapeDtypeStruct((96, 256), BF),
            jax.ShapeDtypeStruct((8, 256), F32),
        ),
        in_specs=[SMEM] + [WHOLE] * 5,
        out_specs=[VMEM] * 4,
        compiler_params=params(60),
        name="coarse_weights",
    )(step_index, ladder, timing_one, turned_inlet, middle_one, outlet_one)
    to_next, to_prev, west, east, bias = lax.optimization_barrier((to_next, to_prev, west, east, bias))
    above = lax.ppermute(to_next, ("row", "col"), shift_pairs(count, 1))
    below = lax.ppermute(to_prev, ("row", "col"), shift_pairs(count, -1))
    blocks = len(starts_of(band + 4, ROWS1))
    deep = LANES + 6 * 8 * (ROWS1 + 2)
    first_two, mid_two, last_two = pl.pallas_call(
        functools.partial(fine_weights, band),
        out_shape=(
            jax.ShapeDtypeStruct((blocks, 32 * ROWS1, deep), BF),
            jax.ShapeDtypeStruct((32 * ROWS2, 768), BF),
            jax.ShapeDtypeStruct((24 * ROWS3, 32 * (ROWS3 + 2)), BF),
        ),
        in_specs=[SMEM] + [WHOLE] * 6,
        out_specs=[VMEM] * 3,
        scratch_shapes=[
            pltpu.VMEM((32 * ROWS1, deep - LANES), F32),
            pltpu.VMEM((32 * ROWS2, 768), F32),
            pltpu.VMEM((24 * ROWS3, 32 * (ROWS3 + 2)), F32),
        ],
        compiler_params=params(60),
        name="fine_weights",
    )(step_index, ladder, timing_two, inlet_two, middle_two, outlet_two, land_bias[:, None])

    px = cols + 2 * EDGE
    pairs = (tile_rows + 8) // 2
    each = tile_rows // col_count
    coarse_next, noise_one, sends = pl.pallas_call(
        functools.partial(coarse_kernel, tile_rows, cols, col_count),
        out_shape=(
            jax.ShapeDtypeStruct((fields * tile_rows, cols), F32),
            jax.ShapeDtypeStruct((fields * tile_rows, cols), F32),
            jax.ShapeDtypeStruct((col_count, (each + 4) * fields, cols), BF),
        ),
        in_specs=[SMEM] + [VMEM] * 11,
        out_specs=[VMEM] * 3,
        scratch_shapes=[
            pltpu.VMEM((-(-pairs // 3), px, 3 * LANES), BF),
            pltpu.VMEM((pairs, px, 256), BF),
            pltpu.VMEM((pairs, px, 768), BF),
            pltpu.VMEM((pairs - 1, px, 256), BF),
            pltpu.VMEM((pairs - 1, 96, px), F32),
        ],
        compiler_params=params(60),
        name="coarse",
    )(
        step_index, north, south, tile, west, east, state, first_one, mid_one, last_one, bias,
        scale_one[None, :],
    )

    arrived = lax.all_to_all(sends, "col", split_axis=0, concat_axis=0, tiled=True)

    fine_next, noise_two = pl.pallas_call(
        functools.partial(fine_kernel, band, quarter),
        out_shape=(
            jax.ShapeDtypeStruct((fields, band, width), F32),
            jax.ShapeDtypeStruct((fields, band, width), F32),
        ),
        in_specs=[SMEM] + [VMEM, ANY] + [VMEM] * 8,
        out_specs=[ANY] * 2,
        scratch_shapes=[
            pltpu.VMEM(((band + 6) * 8, quarter), F32),
            pltpu.VMEM((6, (band + 6) * 8, quarter), BF),
            pltpu.VMEM((6, (band + 6) * 8, quarter), BF),
            pltpu.VMEM((6, 32, quarter), BF),
            pltpu.VMEM((6, (band + 4) * 32, quarter), BF),
            pltpu.VMEM((4, (band + 2) * 32, quarter), BF),
            pltpu.VMEM((fields, band, width), F32),
            pltpu.VMEM((fields, band, width), F32),
            pltpu.VMEM((fields, band, width), F32),
            pltpu.SemaphoreType.DMA((1 + 2 * (band // ROWS3),)),
        ],
        compiler_params=params(60),
        name="fine",
    )(
        step_index, arrived, fine_state, own, ground, above, below, jnp.asarray(turn.T, BF),
        first_two, mid_two, last_two,
    )

    return (
        coarse_next.reshape(coarse_state.shape),
        noise_one.reshape(coarse_state.shape),
        fine_next,
        noise_two,
    )


def solution(mesh):
    return jax.shard_map(
        body,
        mesh=mesh,
        in_specs=(
            P(), P(None, "row", "col"), P(None, "row", "col"), P(None, ("row", "col"), None),
            P(("row", "col"), None), P(), P(), P(), P(), P(), P(), P(), P(), P(), P(),
        ),
        out_specs=(
            P(None, "row", "col"), P(None, "row", "col"), P(None, ("row", "col"), None),
            P(None, ("row", "col"), None),
        ),
        check_vma=False,
    )
```

```python
import functools
import math

import jax
import jax.numpy as jnp
import numpy as np
from jax import lax
from jax.experimental import pallas as pl
from jax.experimental.pallas import tpu as pltpu
from jax.sharding import PartitionSpec as P

BF = jnp.bfloat16
F32 = jnp.float32
VMEM = pl.BlockSpec(memory_space=pltpu.VMEM)
SMEM = pl.BlockSpec(memory_space=pltpu.SMEM)
ANY = pl.BlockSpec(memory_space=pl.ANY)
WHOLE = pl.BlockSpec()
EDGE = 16
MARGIN = 8
ROWS1 = 6
ROWS2 = 6
ROWS3 = 8
LANES = 128


def params(mib):
    return pltpu.CompilerParams(vmem_limit_bytes=mib << 20)


def silu(v):
    return v * (0.5 * jnp.tanh(0.5 * v) + 0.5)


def starts_of(rows, height):
    return [min(s, rows - height) for s in range(0, rows, height)]


def shift_pairs(count, by):
    return [(i, (i + by) % count) for i in range(count)]


def alpha_bar(moment):
    return jnp.cos((moment / 1000.0 + 0.008) / 1.008 * (math.pi / 2.0)) ** 2


def plan(step, shape):
    current_time = jnp.full(shape, step.astype(F32), F32)
    current = alpha_bar(current_time)
    earlier = alpha_bar(current_time - 50.0)
    keeping = jnp.sqrt(earlier / current)
    blending = jnp.sqrt(1.0 - earlier) - jnp.sqrt(earlier) * jnp.sqrt(1.0 - current) / jnp.sqrt(
        current
    )
    return (keeping, blending)


def embed(step, ladder, timing):
    half = ladder.shape[1] // 2
    angles = step.astype(F32) * ladder[...]
    lane = lax.broadcasted_iota(jnp.int32, angles.shape, 1)
    feature = jnp.where(lane < half, jnp.sin(angles), jnp.cos(angles))
    parts = []
    for _ in range(3):
        part = feature.astype(BF)
        feature = feature - part.astype(F32)
        parts.append(part)
    return sum(jnp.dot(part, timing, preferred_element_type=F32) for part in parts)


def ladder_rows(width):
    steps = np.exp(-math.log(10000.0) * np.arange(width // 2) / (width // 2))
    return jnp.asarray(np.tile(np.concatenate([steps, steps]), (8, 1)), F32)


def pack_kernel(tile_rows, state, forcing, comb, top, bottom, near, wide, narrow, sems):
    copies = [
        pltpu.make_async_copy(state, near, sems.at[0]),
        pltpu.make_async_copy(forcing, narrow, sems.at[1]),
    ]
    for copy in copies:
        copy.start()
    for copy in copies:
        copy.wait()
    wide[...] = narrow[...].astype(F32)
    for y in range(tile_rows):
        made = jnp.concatenate(
            [near[pl.ds(y, 8, stride=tile_rows), :], wide[pl.ds(y, 8, stride=tile_rows), :]], axis=0
        ).astype(BF)
        comb[y] = made
        if y < 5:
            top[y] = made
        if y >= tile_rows - 5:
            bottom[y - tile_rows + 5] = made


def edge_kernel(tile_rows, north, comb, south, tile, first_cols, last_cols):
    cols = comb.shape[2]

    def row(e):
        if e < 5:
            return north[e]
        return comb[e - 5] if e < tile_rows + 5 else south[min(e - tile_rows - 5, 4)]

    for g in range(tile.shape[1] // LANES):
        block = jnp.concatenate([row(6 * g + i).astype(F32) for i in range(8)], axis=0)
        turned = block.T.astype(BF)
        at = slice(g * LANES, (g + 1) * LANES)
        tile[:, at] = turned
        first_cols[:, at] = turned[0:EDGE]
        last_cols[:, at] = turned[cols - EDGE :]


def sort_kernel(fine, land, turn, order, own, ground, to_next, to_prev):
    blocks = []
    for m in range(fine.shape[1] // (4 * LANES)):
        cols = slice(4 * LANES * m, 4 * LANES * (m + 1))
        blocks += [fine[:, cols], land[:, cols].astype(F32)]
    high = fine.shape[0] + land.shape[0]
    sorted_all = jnp.dot(
        jnp.concatenate(blocks, axis=0).astype(BF), turn[...], preferred_element_type=F32
    )
    for m in range(fine.shape[1] // (4 * LANES)):
        block = sorted_all[m * high : (m + 1) * high].astype(BF)
        made = jnp.dot(order[...], block, preferred_element_type=F32).astype(BF)
        at = slice(m * LANES, (m + 1) * LANES)
        for j in range(4):
            part = made[:, j * LANES : (j + 1) * LANES]
            to_next[j, :, at] = part[0:32]
            to_prev[j, :, at] = part[32:64]
            ground[j, :, at] = part[64:80]
            own[j, :, at] = part[80:]


def ground_row(band, e):
    if e < 3:
        return 21 + e
    return e - 3 if e < band + 3 else 24 + e - band - 3


def coarse_weights(
    steps, ladder, timing, inlet_one, middle_one, outlet_one, first_one, mid_one, last_one, bias,
):
    made = embed(steps[0], ladder, timing[...])
    bias[...] = jnp.concatenate([made, made], axis=1)
    first_one[...] = jnp.zeros_like(first_one)
    for t in range(3):
        for dx in range(3):
            for i in range(2):
                for dy in range(3):
                    at = dx * LANES + (2 * t + i + dy) * 16
                    first_one[t, at : at + 16, i * 128 : (i + 1) * 128] = inlet_one[dy, dx]
    mid_one[...] = jnp.zeros_like(mid_one)
    last_one[...] = jnp.zeros_like(last_one)
    for dx in range(3):
        for dy in range(3):
            turned = middle_one[dy, dx].astype(F32).T.astype(BF)
            for i in range(2):
                at = dx * 512 + (i + dy) * 128
                mid_one[at : at + 128, i * 128 : (i + 1) * 128] = turned
    for dx in range(3):
        for slot in range(2):
            pieces = []
            for i in range(2):
                halves = []
                for par in range(2):
                    dy = 2 * slot + par - i
                    halves.append(
                        outlet_one[dy, dx].astype(F32) if 0 <= dy <= 2 else jnp.zeros((8, 128), F32)
                    )
                pieces.append(jnp.concatenate(halves, axis=1))
            at = dx * 32 + slot * 16
            last_one[at : at + 16, :] = jnp.concatenate(pieces, axis=0).astype(BF)


def fine_weights(
    band, steps, ladder, timing, inlet_two, middle_two, outlet_two, land_bias, first_two, mid_two, last_two,
    wide1, wide2, wide3,
):
    bias_two = embed(steps[1], ladder, timing[...])[0:1].T
    wide1[...] = jnp.zeros_like(wide1)
    wide2[...] = jnp.zeros_like(wide2)
    wide3[...] = jnp.zeros_like(wide3)
    span = (ROWS1 + 2) * 8
    for dx in range(3):
        for dy in range(3):
            w1 = inlet_two[dy, dx].astype(F32)[:, :16]
            w2 = middle_two[dy, dx].astype(F32)
            for i in range(ROWS1):
                for half in range(2):
                    at = (3 * half + dx) * span + (i + dy) * 8
                    wide1[32 * i : 32 * i + 32, at : at + 8] = w1[:, 8 * half : 8 * half + 8]
            for i in range(ROWS2):
                at = dx * 256 + (i + dy) * 32
                wide2[32 * i : 32 * i + 32, at : at + 32] = w2
    columns = lax.broadcasted_iota(jnp.int32, (ROWS3, 32 * (ROWS3 + 2)), 1)
    offset = columns // 32 - lax.broadcasted_iota(jnp.int32, columns.shape, 0)
    for dx in range(3):
        for o in range(8):
            value = jnp.zeros(columns.shape, F32)
            for dy in range(3):
                line = outlet_two[dy, dx].astype(F32)[o : o + 1]
                line = jnp.concatenate([line] * (ROWS3 + 2), axis=1)
                value = jnp.where(offset == dy, line, value)
            row = (dx * 8 + o) * ROWS3
            wide3[row : row + ROWS3, :] = value
    mid_two[...] = wide2[...].astype(BF)
    last_two[...] = wide3[...].astype(BF)
    lane = lax.broadcasted_iota(jnp.int32, (32, LANES), 1)

    def spread(column):
        return jnp.broadcast_to(column, (32, LANES))

    def split(value):
        high = value.astype(BF).astype(F32)
        return high, (value - high).astype(BF).astype(F32)

    taps = [[spread(inlet_two[dy, dx].astype(F32)[:, 16:17]) for dx in range(3)] for dy in range(3)]
    centre_high, centre_low = split(taps[1][1] + spread(land_bias[...]))
    taps[1][1] = centre_high
    bias_high, bias_low = split(spread(bias_two))
    starts = starts_of(band + 4, ROWS1)
    for b, s in enumerate(starts):
        for i in range(ROWS1):
            value = jnp.where(lane == 48, bias_high, 0.0)
            value = jnp.where(lane == 49, bias_low, value)
            for dx in range(3):
                for dy in range(3):
                    value = jnp.where(lane == dx * 32 + ground_row(band, s + i + dy), taps[dy][dx], value)
            value = jnp.where(lane == 96 + ground_row(band, s + i + 1), centre_low, value)
            first_two[b, 32 * i : 32 * i + 32, 0:LANES] = value.astype(BF)
        first_two[b, :, LANES:] = wide1[...].astype(BF)


def coarse_kernel(
    tile_rows, cols, dests, steps, north, south, own, west, east, state, first_one, mid_one, last_one,
    bias, scale, coarse_next, noise_one, sends, turned, hidden, active, summed, taps,
):
    px = cols + 2 * MARGIN
    rows_before, cols_before = lax.axis_index("row") * tile_rows, lax.axis_index("col") * cols
    rows_total, cols_total = lax.axis_size("row") * tile_rows, lax.axis_size("col") * cols
    keep, blend = plan(steps[0], (8, cols))
    ext = tile_rows + 10
    pairs = (tile_rows + 8) // 2
    column = cols_before - MARGIN + lax.broadcasted_iota(jnp.int32, (px, 256), 0)
    half = lax.broadcasted_iota(jnp.int32, (px, 256), 1) // 128
    inside = jnp.where((column >= 0) & (column < cols_total), 1.0, 0.0)

    gains = jnp.concatenate([scale[...], scale[...]], axis=1)
    for g in range(-(-pairs // 3)):
        lanes = slice(g * LANES, (g + 1) * LANES)
        sides = [ref[:, lanes].astype(F32) for ref in (west, own, east)]
        whole = jnp.concatenate(
            [sides[0][EDGE - MARGIN :], sides[1], sides[2][:MARGIN]], axis=0
        )
        row = rows_before - 5 + 6 * g + lax.broadcasted_iota(jnp.int32, (px, LANES), 1) // 16
        whole = jnp.where((row >= 0) & (row < rows_total) & (inside[:, 0:LANES] > 0), whole, 0.0)
        turned[g, :, 0:LANES] = pltpu.roll(whole, 1, 0).astype(BF)
        turned[g, :, LANES : 2 * LANES] = whole.astype(BF)
        turned[g, :, 2 * LANES :] = pltpu.roll(whole, px - 1, 0).astype(BF)

    def mask(first_row):
        row = rows_before - 5 + first_row + half
        return jnp.where((row >= 0) & (row < rows_total), inside, 0.0)

    for p in range(pairs):
        acc = jnp.dot(turned[p // 3], first_one[p % 3], preferred_element_type=F32)
        low = silu(acc + bias[0:1, :]).astype(BF)
        hidden[p] = low
        value = low.astype(F32)
        square = value * value
        scaled = []
        for h in range(2):
            mean = jnp.mean(square[:, h * 128 : (h + 1) * 128], axis=1, keepdims=True)
            scaled.append(value[:, h * 128 : (h + 1) * 128] * lax.rsqrt(mean + 1e-06))
        act = silu(jnp.concatenate(scaled, axis=1) * gains) * mask(1 + 2 * p)
        active[p, :, 0:256] = pltpu.roll(act, 1, 0).astype(BF)
        active[p, :, 256:512] = act.astype(BF)
        active[p, :, 512:768] = pltpu.roll(act, px - 1, 0).astype(BF)

    for p in range(0, pairs - 1, 2):
        size = min(2, pairs - 1 - p)
        parts = [
            active[p + q : p + q + size, :, dx * 256 : (dx + 1) * 256].reshape(size * px, 256)
            for dx in range(3)
            for q in range(2)
        ]
        acc = jnp.dot(jnp.concatenate(parts, axis=1), mid_one[...], preferred_element_type=F32)
        for k in range(size):
            n = p + k
            rest = jnp.concatenate([hidden[n, :, 128:256], hidden[n + 1, :, 0:128]], axis=1)
            value = acc[k * px : (k + 1) * px] + rest.astype(F32)
            summed[n] = (value * mask(2 + 2 * n)).astype(BF)

    for p in range(pairs - 1):
        taps[p] = lax.dot_general(
            last_one[...], summed[p], (((1,), (1,)), ((), ())), preferred_element_type=F32
        )
    each = tile_rows // dests
    for p in range(pairs - 2):
        noise = None
        for dx in range(3):
            at = MARGIN - 1 + dx
            term = (
                taps[p, dx * 32 : dx * 32 + 16, at : at + cols]
                + taps[p + 1, dx * 32 + 16 : dx * 32 + 32, at : at + cols]
            )
            noise = term if noise is None else noise + term
        made = []
        for i in range(2):
            y = 2 * p - 2 + i
            part = noise[8 * i : 8 * i + 8]
            if 0 <= y < tile_rows:
                rows = pl.ds(y, 8, stride=tile_rows)
                after = keep * state[rows, :] + blend * part
                noise_one[rows, :] = part
                coarse_next[rows, :] = after
            else:
                edge = north[y + 5] if y < 0 else south[y - tile_rows]
                after = keep * edge.astype(F32)[0:8] + blend * part
            made.append(after)
        made = jnp.concatenate(made, axis=0).astype(BF)
        for d in range(dests):
            slot = 2 * p - each * d
            if 0 <= slot < each + 4:
                sends[d, slot * 8 : slot * 8 + 16, :] = made


def fine_kernel(
    band, quarter, steps, coarse, fine_far, own, land, above, below, back, first_two, mid_two, last_two,
    fine_far_next, noise_far, rows_of, states, lifted, ground, hidden, summed, fine, fine_next, noise_two, sems,
):
    bring = pltpu.make_async_copy(fine_far, fine, sems.at[0])
    bring.start()
    keep, blend = plan(steps[1], (8, LANES))
    keep, blend = (jnp.concatenate([v] * 4, axis=1) for v in (keep, blend))
    position = lax.axis_index("row") * lax.axis_size("col") + lax.axis_index("col")
    count = lax.axis_size("row") * lax.axis_size("col")
    top = jnp.where(position > 0, 1.0, 0.0)
    bottom = jnp.where(position < count - 1, 1.0, 0.0)
    ext = band + 6
    quota = band // 4
    sources = quarter // LANES
    tall = ext * 8

    def edge(value, by):
        lane = lax.broadcasted_iota(jnp.int32, value.shape, 1)
        if by > 0:
            return jnp.where(lane == 0, 0.0, pltpu.roll(value, 1, 1))
        return jnp.where(lane == quarter - 1, 0.0, pltpu.roll(value, quarter - 1, 1))

    def keep_phase(ref, j, rows, value):
        ref[j + 1, rows, :] = value.astype(BF)
        if j == 0:
            ref[5, rows, :] = edge(value, -1).astype(BF)
        if j == 3:
            ref[0, rows, :] = edge(value, 1).astype(BF)

    field = lax.broadcasted_iota(jnp.int32, (16, quarter), 0)
    for j in range(4):
        upper = above[j].astype(F32) * top
        lower = below[j].astype(F32) * bottom
        mine = own[j].astype(F32)
        high = jnp.where(field < 8, upper[16:32], mine[0:16])
        low = jnp.where(field < 8, mine[tall - 48 :], lower[0:16])
        keep_phase(
            states, j, slice(0, tall),
            jnp.concatenate([upper[0:16], high, mine[16 : tall - 48], low, lower[16:32]], axis=0),
        )
        tail = jnp.concatenate([upper[24:32], lower[0:8]], axis=0)
        tail = jnp.where(field < 2, 1.0, tail)
        keep_phase(
            ground, j, slice(0, 32), jnp.concatenate([land[j].astype(F32), tail], axis=0)
        )

    for m in range(sources):
        block = coarse[m].astype(F32)
        rows = [block[8 * j : 8 * j + 8] for j in range(quota + 4)]
        rows[1] = top * rows[1] + (1.0 - top) * rows[2]
        rows[quota + 2] = bottom * rows[quota + 2] + (1.0 - bottom) * rows[quota + 1]
        for e in range(ext):
            k, phase = divmod(e - 3, 4)
            j = k + 2
            other, near, far = (
                (j - 1, 0.625, 0.375), (j - 1, 0.875, 0.125), (j + 1, 0.875, 0.125), (j + 1, 0.625, 0.375),
            )[phase]
            value = near * rows[j] + far * rows[other]
            if e < 3:
                value = value * top
            if e >= band + 3:
                value = value * bottom
            rows_of[8 * e : 8 * e + 8, m * LANES : (m + 1) * LANES] = value
    centre = rows_of[...]
    lane = lax.broadcasted_iota(jnp.int32, centre.shape, 1)
    before = jnp.where(lane == 0, centre, pltpu.roll(centre, 1, 1))
    after = jnp.where(lane == quarter - 1, centre, pltpu.roll(centre, quarter - 1, 1))
    for j, (side, near, far) in enumerate(
        ((before, 0.625, 0.375), (before, 0.875, 0.125), (after, 0.875, 0.125), (after, 0.625, 0.375))
    ):
        keep_phase(lifted, j, slice(0, tall), near * centre + far * side)

    done = 0
    for b, s in enumerate(starts_of(band + 4, ROWS1)):
        for j in range(4):
            window = slice(8 * s, 8 * (s + ROWS1 + 2))
            operand = [ground[j], ground[j + 1], ground[j + 2], ground[j + 1]]
            operand += [states[j + k, window] for k in range(3)]
            operand += [lifted[j + k, window] for k in range(3)]
            value = jnp.dot(
                first_two[b], jnp.concatenate(operand, axis=0), preferred_element_type=F32
            )[32 * (done - s) :]
            value = silu(value)
            parts = []
            for i in range(done, s + ROWS1):
                part = value[32 * (i - done) : 32 * (i - done) + 32]
                if i < 2:
                    part = part * top
                if i >= band + 2:
                    part = part * bottom
                parts.append(part)
            keep_phase(hidden, j, slice(32 * done, 32 * (s + ROWS1)), jnp.concatenate(parts, axis=0))
        done = s + ROWS1

    done = 0
    for s in starts_of(band + 2, ROWS2):
        for j in range(4):
            window = slice(32 * s, 32 * (s + ROWS2 + 2))
            value = jnp.dot(
                mid_two[...], jnp.concatenate([hidden[j + k, window] for k in range(3)], axis=0),
                preferred_element_type=F32,
            )
            for i in range(done, s + ROWS2):
                rows = slice(32 * (i + 1), 32 * (i + 2))
                part = value[32 * (i - s) : 32 * (i - s) + 32] + hidden[j + 1, rows].astype(F32)
                if i < 1:
                    part = part * top
                if i >= band + 1:
                    part = part * bottom
                summed[j, 32 * i : 32 * i + 32] = part.astype(BF)
        done = s + ROWS2

    high = 8 * ROWS3
    bring.wait()
    sends = []
    for s in range(0, band, ROWS3):
        made = [
            jnp.dot(last_two[...], summed[j, 32 * s : 32 * (s + ROWS3 + 2)], preferred_element_type=F32)
            for j in range(4)
        ]
        west = [edge(made[3][0:high], 1)] + [made[j][0:high] for j in range(3)]
        east = [made[j][2 * high :] for j in range(1, 4)] + [edge(made[0][2 * high :], -1)]
        phases = [west[j] + made[j][high : 2 * high] + east[j] for j in range(4)]
        value = jnp.concatenate(
            [
                jnp.concatenate([p[:, m * LANES : (m + 1) * LANES] for p in phases], axis=1)
                for m in range(sources)
            ],
            axis=0,
        )
        back_all = jnp.dot(value.astype(BF), back[...], preferred_element_type=F32)
        for m in range(sources):
            noise = back_all[m * high : (m + 1) * high]
            cols = slice(4 * LANES * m, 4 * LANES * (m + 1))
            for o in range(8):
                rows = slice(s, s + ROWS3)
                part = noise[ROWS3 * o : ROWS3 * o + ROWS3]
                noise_two[o, rows, cols] = part
                fine_next[o, rows, cols] = keep * fine[o, rows, cols] + blend * part
            if m % 2 == 1:
                there = (slice(None), pl.ds(s, ROWS3), pl.ds(4 * LANES * (m - 1), 8 * LANES))
                for near, far in ((noise_two, noise_far), (fine_next, fine_far_next)):
                    sem = sems.at[1 + len(sends)]
                    sends.append(pltpu.make_async_copy(near.at[there], far.at[there], sem))
                    sends[-1].start()
    for send in sends:
        send.wait()


def turn_matrix():
    made = np.zeros((4 * LANES, 4 * LANES))
    for n in range(4 * LANES):
        made[n, (n % 4) * LANES + n // 4] = 1
    return made


def order_matrix(band):
    made = np.zeros((80 + 8 * (band + 2), 9 * band))
    for o in range(8):
        for y in range(3):
            made[8 * y + o, o * band + band - 3 + y] = 1
            made[32 + 8 * (y + 1) + o, o * band + y] = 1
        for y in range(band):
            made[80 + 8 * (y + 1) + o, o * band + y] = 1
    for y in range(8):
        made[24 + y, 8 * band + band - 8 + y] = 1
        made[32 + y, 8 * band + y] = 1
    for y in range(band):
        made[64 + y, 8 * band + y] = 1
    return made


def body(
    step_index, coarse_state, coarse_forcing, fine_state, land_mask, inlet_one, timing_one, scale_one,
    middle_one, outlet_one, inlet_two, timing_two, land_bias, middle_two, outlet_two,
):
    fields, tile_rows, cols = coarse_state.shape
    _, band, width = fine_state.shape
    row_count, col_count = lax.axis_size("row"), lax.axis_size("col")
    count = row_count * col_count
    state = coarse_state.reshape(fields * tile_rows, cols)
    forcing = coarse_forcing.reshape(fields * tile_rows, cols)
    fine = fine_state.reshape(fields * band, width)
    quarter = width // 4
    ladder = ladder_rows(timing_one.shape[0])

    comb, first_rows, last_rows = pl.pallas_call(
        functools.partial(pack_kernel, tile_rows),
        out_shape=(
            jax.ShapeDtypeStruct((tile_rows, 2 * fields, cols), BF),
            jax.ShapeDtypeStruct((5, 2 * fields, cols), BF),
            jax.ShapeDtypeStruct((5, 2 * fields, cols), BF),
        ),
        in_specs=[ANY] * 2,
        out_specs=[VMEM] * 3,
        scratch_shapes=[
            pltpu.VMEM((fields * tile_rows, cols), F32),
            pltpu.VMEM((fields * tile_rows, cols), F32),
            pltpu.VMEM((fields * tile_rows, cols), BF),
            pltpu.SemaphoreType.DMA((2,)),
        ],
        compiler_params=params(60),
        name="pack",
    )(state, forcing)
    north = lax.ppermute(last_rows, "row", shift_pairs(row_count, 1))
    south = lax.ppermute(first_rows, "row", shift_pairs(row_count, -1))

    turn = turn_matrix()
    split = 2048
    part = split // 4
    shapes = (8 * (band + 2), 16, 32, 32)
    own, ground, to_next, to_prev = pl.pallas_call(
        sort_kernel,
        grid=(width // split,),
        out_shape=[jax.ShapeDtypeStruct((4, rows, quarter), BF) for rows in shapes],
        in_specs=[
            pl.BlockSpec((fields * band, split), lambda n: (0, n)),
            pl.BlockSpec((band, split), lambda n: (0, n)),
            pl.BlockSpec((4 * LANES, 4 * LANES), lambda n: (0, 0)),
            pl.BlockSpec((80 + 8 * (band + 2), 9 * band), lambda n: (0, 0)),
        ],
        out_specs=[pl.BlockSpec((4, rows, part), lambda n: (0, 0, n)) for rows in shapes],
        compiler_params=params(60),
        name="sort",
    )(fine, land_mask, jnp.asarray(turn, BF), jnp.asarray(order_matrix(band), BF))
    north, to_next, to_prev = lax.optimization_barrier((north, to_next, to_prev))
    deep_rows = -(-(tile_rows + 8) // 6) * LANES
    tile, first_cols, last_cols = pl.pallas_call(
        functools.partial(edge_kernel, tile_rows),
        out_shape=(
            jax.ShapeDtypeStruct((cols, deep_rows), BF),
            jax.ShapeDtypeStruct((EDGE, deep_rows), BF),
            jax.ShapeDtypeStruct((EDGE, deep_rows), BF),
        ),
        in_specs=[VMEM] * 3,
        out_specs=[VMEM] * 3,
        compiler_params=params(8),
        name="edges",
    )(north, comb, south)
    west = lax.ppermute(last_cols, "col", shift_pairs(col_count, 1))
    east = lax.ppermute(first_cols, "col", shift_pairs(col_count, -1))
    turned_inlet, first_cols = lax.optimization_barrier(
        (jnp.transpose(inlet_one, (0, 1, 3, 2)), first_cols)
    )
    first_one, mid_one, last_one, bias = pl.pallas_call(
        coarse_weights,
        out_shape=(
            jax.ShapeDtypeStruct((3, 3 * LANES, 256), BF),
            jax.ShapeDtypeStruct((1536, 256), BF),
            jax.ShapeDtypeStruct((96, 256), BF),
            jax.ShapeDtypeStruct((8, 256), F32),
        ),
        in_specs=[SMEM] + [WHOLE] * 5,
        out_specs=[VMEM] * 4,
        compiler_params=params(60),
        name="coarse_weights",
    )(step_index, ladder, timing_one, turned_inlet, middle_one, outlet_one)
    to_next, to_prev, west, east, bias = lax.optimization_barrier((to_next, to_prev, west, east, bias))
    above = lax.ppermute(to_next, ("row", "col"), shift_pairs(count, 1))
    below = lax.ppermute(to_prev, ("row", "col"), shift_pairs(count, -1))
    blocks = len(starts_of(band + 4, ROWS1))
    deep = LANES + 6 * 8 * (ROWS1 + 2)
    first_two, mid_two, last_two = pl.pallas_call(
        functools.partial(fine_weights, band),
        out_shape=(
            jax.ShapeDtypeStruct((blocks, 32 * ROWS1, deep), BF),
            jax.ShapeDtypeStruct((32 * ROWS2, 768), BF),
            jax.ShapeDtypeStruct((24 * ROWS3, 32 * (ROWS3 + 2)), BF),
        ),
        in_specs=[SMEM] + [WHOLE] * 6,
        out_specs=[VMEM] * 3,
        scratch_shapes=[
            pltpu.VMEM((32 * ROWS1, deep - LANES), F32),
            pltpu.VMEM((32 * ROWS2, 768), F32),
            pltpu.VMEM((24 * ROWS3, 32 * (ROWS3 + 2)), F32),
        ],
        compiler_params=params(60),
        name="fine_weights",
    )(step_index, ladder, timing_two, inlet_two, middle_two, outlet_two, land_bias[:, None])

    px = cols + 2 * MARGIN
    pairs = (tile_rows + 8) // 2
    each = tile_rows // col_count
    coarse_next, noise_one, sends = pl.pallas_call(
        functools.partial(coarse_kernel, tile_rows, cols, col_count),
        out_shape=(
            jax.ShapeDtypeStruct((fields * tile_rows, cols), F32),
            jax.ShapeDtypeStruct((fields * tile_rows, cols), F32),
            jax.ShapeDtypeStruct((col_count, (each + 4) * fields, cols), BF),
        ),
        in_specs=[SMEM] + [VMEM] * 11,
        out_specs=[VMEM] * 3,
        scratch_shapes=[
            pltpu.VMEM((-(-pairs // 3), px, 3 * LANES), BF),
            pltpu.VMEM((pairs, px, 256), BF),
            pltpu.VMEM((pairs, px, 768), BF),
            pltpu.VMEM((pairs - 1, px, 256), BF),
            pltpu.VMEM((pairs - 1, 96, px), F32),
        ],
        compiler_params=params(60),
        name="coarse",
    )(
        step_index, north, south, tile, west, east, state, first_one, mid_one, last_one, bias,
        scale_one[None, :],
    )

    arrived = lax.all_to_all(sends, "col", split_axis=0, concat_axis=0, tiled=True)

    fine_next, noise_two = pl.pallas_call(
        functools.partial(fine_kernel, band, quarter),
        out_shape=(
            jax.ShapeDtypeStruct((fields, band, width), F32),
            jax.ShapeDtypeStruct((fields, band, width), F32),
        ),
        in_specs=[SMEM] + [VMEM, ANY] + [VMEM] * 8,
        out_specs=[ANY] * 2,
        scratch_shapes=[
            pltpu.VMEM(((band + 6) * 8, quarter), F32),
            pltpu.VMEM((6, (band + 6) * 8, quarter), BF),
            pltpu.VMEM((6, (band + 6) * 8, quarter), BF),
            pltpu.VMEM((6, 32, quarter), BF),
            pltpu.VMEM((6, (band + 4) * 32, quarter), BF),
            pltpu.VMEM((4, (band + 2) * 32, quarter), BF),
            pltpu.VMEM((fields, band, width), F32),
            pltpu.VMEM((fields, band, width), F32),
            pltpu.VMEM((fields, band, width), F32),
            pltpu.SemaphoreType.DMA((1 + (band // ROWS3) * (quarter // LANES),)),
        ],
        compiler_params=params(60),
        name="fine",
    )(
        step_index, arrived, fine_state, own, ground, above, below, jnp.asarray(turn.T, BF),
        first_two, mid_two, last_two,
    )

    return (
        coarse_next.reshape(coarse_state.shape),
        noise_one.reshape(coarse_state.shape),
        fine_next,
        noise_two,
    )


def solution(mesh):
    return jax.shard_map(
        body,
        mesh=mesh,
        in_specs=(
            P(), P(None, "row", "col"), P(None, "row", "col"), P(None, ("row", "col"), None),
            P(("row", "col"), None), P(), P(), P(), P(), P(), P(), P(), P(), P(), P(),
        ),
        out_specs=(
            P(None, "row", "col"), P(None, "row", "col"), P(None, ("row", "col"), None),
            P(None, ("row", "col"), None),
        ),
        check_vma=False,
    )
```

```python
import functools
import math

import jax
import jax.numpy as jnp
import numpy as np
from jax import lax
from jax.experimental import pallas as pl
from jax.experimental.pallas import tpu as pltpu
from jax.sharding import PartitionSpec as P

BF = jnp.bfloat16
F32 = jnp.float32
VMEM = pl.BlockSpec(memory_space=pltpu.VMEM)
SMEM = pl.BlockSpec(memory_space=pltpu.SMEM)
ANY = pl.BlockSpec(memory_space=pl.ANY)
WHOLE = pl.BlockSpec()
EDGE = 16
MARGIN = 8
ROWS1 = 6
ROWS2 = 6
ROWS3 = 8
LANES = 128


def params(mib):
    return pltpu.CompilerParams(vmem_limit_bytes=mib << 20)


def silu(v):
    return v * (0.5 * jnp.tanh(0.5 * v) + 0.5)


def starts_of(rows, height):
    return [min(s, rows - height) for s in range(0, rows, height)]


def shift_pairs(count, by):
    return [(i, (i + by) % count) for i in range(count)]


def alpha_bar(moment):
    return jnp.cos((moment / 1000.0 + 0.008) / 1.008 * (math.pi / 2.0)) ** 2


def plan(step, shape):
    current_time = jnp.full(shape, step.astype(F32), F32)
    current = alpha_bar(current_time)
    earlier = alpha_bar(current_time - 50.0)
    keeping = jnp.sqrt(earlier / current)
    blending = jnp.sqrt(1.0 - earlier) - jnp.sqrt(earlier) * jnp.sqrt(1.0 - current) / jnp.sqrt(
        current
    )
    return (keeping, blending)


def embed(step, ladder, timing):
    half = ladder.shape[1] // 2
    angles = step.astype(F32) * ladder[...]
    lane = lax.broadcasted_iota(jnp.int32, angles.shape, 1)
    feature = jnp.where(lane < half, jnp.sin(angles), jnp.cos(angles))
    parts = []
    for _ in range(3):
        part = feature.astype(BF)
        feature = feature - part.astype(F32)
        parts.append(part)
    return sum(jnp.dot(part, timing, preferred_element_type=F32) for part in parts)


def ladder_rows(width):
    steps = np.exp(-math.log(10000.0) * np.arange(width // 2) / (width // 2))
    return jnp.asarray(np.tile(np.concatenate([steps, steps]), (8, 1)), F32)


def pack_kernel(tile_rows, state, forcing, comb, top, bottom, near, wide, narrow, sems):
    copies = [
        pltpu.make_async_copy(state, near, sems.at[0]),
        pltpu.make_async_copy(forcing, narrow, sems.at[1]),
    ]
    for copy in copies:
        copy.start()
    for copy in copies:
        copy.wait()
    wide[...] = narrow[...].astype(F32)
    for y in range(tile_rows):
        made = jnp.concatenate(
            [near[pl.ds(y, 8, stride=tile_rows), :], wide[pl.ds(y, 8, stride=tile_rows), :]], axis=0
        ).astype(BF)
        comb[y] = made
        if y < 5:
            top[y] = made
        if y >= tile_rows - 5:
            bottom[y - tile_rows + 5] = made


def edge_kernel(tile_rows, north, comb, south, tile, first_cols, last_cols):
    cols = comb.shape[2]

    def row(e):
        if e < 5:
            return north[e]
        return comb[e - 5] if e < tile_rows + 5 else south[min(e - tile_rows - 5, 4)]

    for g in range(tile.shape[1] // LANES):
        block = jnp.concatenate([row(6 * g + i).astype(F32) for i in range(8)], axis=0)
        turned = block.T.astype(BF)
        at = slice(g * LANES, (g + 1) * LANES)
        tile[:, at] = turned
        first_cols[:, at] = turned[0:EDGE]
        last_cols[:, at] = turned[cols - EDGE :]


def sort_kernel(fine, land, turn, order, own, ground, to_next, to_prev):
    blocks = []
    for m in range(fine.shape[1] // (4 * LANES)):
        cols = slice(4 * LANES * m, 4 * LANES * (m + 1))
        blocks += [fine[:, cols], land[:, cols].astype(F32)]
    high = fine.shape[0] + land.shape[0]
    sorted_all = jnp.dot(
        jnp.concatenate(blocks, axis=0).astype(BF), turn[...], preferred_element_type=F32
    )
    for m in range(fine.shape[1] // (4 * LANES)):
        block = sorted_all[m * high : (m + 1) * high].astype(BF)
        made = jnp.dot(order[...], block, preferred_element_type=F32).astype(BF)
        at = slice(m * LANES, (m + 1) * LANES)
        for j in range(4):
            part = made[:, j * LANES : (j + 1) * LANES]
            to_next[j, :, at] = part[0:32]
            to_prev[j, :, at] = part[32:64]
            ground[j, :, at] = part[64:80]
            own[j, :, at] = part[80:]


def ground_row(band, e):
    if e < 3:
        return 21 + e
    return e - 3 if e < band + 3 else 24 + e - band - 3


def coarse_weights(
    steps, ladder, timing, inlet_one, middle_one, outlet_one, first_one, mid_one, last_one, bias,
):
    made = embed(steps[0], ladder, timing[...])
    bias[...] = jnp.concatenate([made, made], axis=1)
    first_one[...] = jnp.zeros_like(first_one)
    for t in range(3):
        for dx in range(3):
            for i in range(2):
                for dy in range(3):
                    at = dx * LANES + (2 * t + i + dy) * 16
                    first_one[t, at : at + 16, i * 128 : (i + 1) * 128] = inlet_one[dy, dx]
    mid_one[...] = jnp.zeros_like(mid_one)
    last_one[...] = jnp.zeros_like(last_one)
    for dx in range(3):
        for dy in range(3):
            turned = middle_one[dy, dx].astype(F32).T.astype(BF)
            for i in range(2):
                at = dx * 512 + (i + dy) * 128
                mid_one[at : at + 128, i * 128 : (i + 1) * 128] = turned
    for dx in range(3):
        for slot in range(2):
            pieces = []
            for i in range(2):
                halves = []
                for par in range(2):
                    dy = 2 * slot + par - i
                    halves.append(
                        outlet_one[dy, dx].astype(F32) if 0 <= dy <= 2 else jnp.zeros((8, 128), F32)
                    )
                pieces.append(jnp.concatenate(halves, axis=1))
            at = dx * 32 + slot * 16
            last_one[at : at + 16, :] = jnp.concatenate(pieces, axis=0).astype(BF)


def fine_weights(
    band, steps, ladder, timing, inlet_two, middle_two, outlet_two, land_bias, first_two, mid_two, last_two,
    wide1, wide2, wide3,
):
    bias_two = embed(steps[1], ladder, timing[...])[0:1].T
    wide1[...] = jnp.zeros_like(wide1)
    wide2[...] = jnp.zeros_like(wide2)
    wide3[...] = jnp.zeros_like(wide3)
    span = (ROWS1 + 2) * 8
    for dx in range(3):
        for dy in range(3):
            w1 = inlet_two[dy, dx].astype(F32)[:, :16]
            w2 = middle_two[dy, dx].astype(F32)
            for i in range(ROWS1):
                for half in range(2):
                    at = (3 * half + dx) * span + (i + dy) * 8
                    wide1[32 * i : 32 * i + 32, at : at + 8] = w1[:, 8 * half : 8 * half + 8]
            for i in range(ROWS2):
                at = dx * 256 + (i + dy) * 32
                wide2[32 * i : 32 * i + 32, at : at + 32] = w2
    columns = lax.broadcasted_iota(jnp.int32, (ROWS3, 32 * (ROWS3 + 2)), 1)
    offset = columns // 32 - lax.broadcasted_iota(jnp.int32, columns.shape, 0)
    for dx in range(3):
        for o in range(8):
            value = jnp.zeros(columns.shape, F32)
            for dy in range(3):
                line = outlet_two[dy, dx].astype(F32)[o : o + 1]
                line = jnp.concatenate([line] * (ROWS3 + 2), axis=1)
                value = jnp.where(offset == dy, line, value)
            row = (dx * 8 + o) * ROWS3
            wide3[row : row + ROWS3, :] = value
    mid_two[...] = wide2[...].astype(BF)
    last_two[...] = wide3[...].astype(BF)
    lane = lax.broadcasted_iota(jnp.int32, (32, LANES), 1)

    def spread(column):
        return jnp.broadcast_to(column, (32, LANES))

    def split(value):
        high = value.astype(BF).astype(F32)
        return high, (value - high).astype(BF).astype(F32)

    taps = [[spread(inlet_two[dy, dx].astype(F32)[:, 16:17]) for dx in range(3)] for dy in range(3)]
    centre_high, centre_low = split(taps[1][1] + spread(land_bias[...]))
    taps[1][1] = centre_high
    bias_high, bias_low = split(spread(bias_two))
    starts = starts_of(band + 4, ROWS1)
    for b, s in enumerate(starts):
        for i in range(ROWS1):
            value = jnp.where(lane == 48, bias_high, 0.0)
            value = jnp.where(lane == 49, bias_low, value)
            for dx in range(3):
                for dy in range(3):
                    value = jnp.where(lane == dx * 32 + ground_row(band, s + i + dy), taps[dy][dx], value)
            value = jnp.where(lane == 96 + ground_row(band, s + i + 1), centre_low, value)
            first_two[b, 32 * i : 32 * i + 32, 0:LANES] = value.astype(BF)
        first_two[b, :, LANES:] = wide1[...].astype(BF)


def coarse_kernel(
    tile_rows, cols, dests, steps, north, south, own, west, east, state, first_one, mid_one, last_one,
    bias, scale, coarse_next, noise_one, sends, turned, hidden, active, summed, taps,
):
    px = cols + 2 * MARGIN
    rows_before, cols_before = lax.axis_index("row") * tile_rows, lax.axis_index("col") * cols
    rows_total, cols_total = lax.axis_size("row") * tile_rows, lax.axis_size("col") * cols
    keep, blend = plan(steps[0], (8, cols))
    ext = tile_rows + 10
    pairs = (tile_rows + 8) // 2
    column = cols_before - MARGIN + lax.broadcasted_iota(jnp.int32, (px, 256), 0)
    half = lax.broadcasted_iota(jnp.int32, (px, 256), 1) // 128
    inside = jnp.where((column >= 0) & (column < cols_total), 1.0, 0.0)

    gains = jnp.concatenate([scale[...], scale[...]], axis=1)
    for g in range(-(-pairs // 3)):
        lanes = slice(g * LANES, (g + 1) * LANES)
        sides = [ref[:, lanes].astype(F32) for ref in (west, own, east)]
        whole = jnp.concatenate(
            [sides[0][EDGE - MARGIN :], sides[1], sides[2][:MARGIN]], axis=0
        )
        row = rows_before - 5 + 6 * g + lax.broadcasted_iota(jnp.int32, (px, LANES), 1) // 16
        whole = jnp.where((row >= 0) & (row < rows_total) & (inside[:, 0:LANES] > 0), whole, 0.0)
        turned[g, :, 0:LANES] = pltpu.roll(whole, 1, 0).astype(BF)
        turned[g, :, LANES : 2 * LANES] = whole.astype(BF)
        turned[g, :, 2 * LANES :] = pltpu.roll(whole, px - 1, 0).astype(BF)

    def mask(first_row):
        row = rows_before - 5 + first_row + half
        return jnp.where((row >= 0) & (row < rows_total), inside, 0.0)

    for p in range(pairs):
        acc = jnp.dot(turned[p // 3], first_one[p % 3], preferred_element_type=F32)
        low = silu(acc + bias[0:1, :]).astype(BF)
        hidden[p] = low
        value = low.astype(F32)
        square = value * value
        scaled = []
        for h in range(2):
            mean = jnp.mean(square[:, h * 128 : (h + 1) * 128], axis=1, keepdims=True)
            scaled.append(value[:, h * 128 : (h + 1) * 128] * lax.rsqrt(mean + 1e-06))
        act = silu(jnp.concatenate(scaled, axis=1) * gains) * mask(1 + 2 * p)
        active[p, :, 0:256] = pltpu.roll(act, 1, 0).astype(BF)
        active[p, :, 256:512] = act.astype(BF)
        active[p, :, 512:768] = pltpu.roll(act, px - 1, 0).astype(BF)

    for p in range(0, pairs - 1, 2):
        size = min(2, pairs - 1 - p)
        parts = [
            active[p + q : p + q + size, :, dx * 256 : (dx + 1) * 256].reshape(size * px, 256)
            for dx in range(3)
            for q in range(2)
        ]
        acc = jnp.dot(jnp.concatenate(parts, axis=1), mid_one[...], preferred_element_type=F32)
        for k in range(size):
            n = p + k
            rest = jnp.concatenate([hidden[n, :, 128:256], hidden[n + 1, :, 0:128]], axis=1)
            value = acc[k * px : (k + 1) * px] + rest.astype(F32)
            summed[n] = (value * mask(2 + 2 * n)).astype(BF)

    for p in range(pairs - 1):
        taps[p] = lax.dot_general(
            last_one[...], summed[p], (((1,), (1,)), ((), ())), preferred_element_type=F32
        )
    each = tile_rows // dests
    for p in range(pairs - 2):
        noise = None
        for dx in range(3):
            at = MARGIN - 1 + dx
            term = (
                taps[p, dx * 32 : dx * 32 + 16, at : at + cols]
                + taps[p + 1, dx * 32 + 16 : dx * 32 + 32, at : at + cols]
            )
            noise = term if noise is None else noise + term
        made = []
        for i in range(2):
            y = 2 * p - 2 + i
            part = noise[8 * i : 8 * i + 8]
            if 0 <= y < tile_rows:
                rows = pl.ds(y, 8, stride=tile_rows)
                after = keep * state[rows, :] + blend * part
                noise_one[rows, :] = part
                coarse_next[rows, :] = after
            else:
                edge = north[y + 5] if y < 0 else south[y - tile_rows]
                after = keep * edge.astype(F32)[0:8] + blend * part
            made.append(after)
        made = jnp.concatenate(made, axis=0).astype(BF)
        for d in range(dests):
            slot = 2 * p - each * d
            if 0 <= slot < each + 4:
                sends[d, slot * 8 : slot * 8 + 16, :] = made


def fine_kernel(
    band, quarter, steps, coarse, fine_far, own, land, above, below, back, first_two, mid_two, last_two,
    fine_far_next, noise_far, rows_of, states, lifted, ground, hidden, summed, fine, fine_next, noise_two, sems,
):
    bring = pltpu.make_async_copy(fine_far, fine, sems.at[0])
    bring.start()
    keep, blend = plan(steps[1], (8, LANES))
    keep, blend = (jnp.concatenate([v] * 4, axis=1) for v in (keep, blend))
    position = lax.axis_index("row") * lax.axis_size("col") + lax.axis_index("col")
    count = lax.axis_size("row") * lax.axis_size("col")
    top = jnp.where(position > 0, 1.0, 0.0)
    bottom = jnp.where(position < count - 1, 1.0, 0.0)
    ext = band + 6
    quota = band // 4
    sources = quarter // LANES
    tall = ext * 8

    def edge(value, by):
        lane = lax.broadcasted_iota(jnp.int32, value.shape, 1)
        if by > 0:
            return jnp.where(lane == 0, 0.0, pltpu.roll(value, 1, 1))
        return jnp.where(lane == quarter - 1, 0.0, pltpu.roll(value, quarter - 1, 1))

    def keep_phase(ref, j, rows, value):
        ref[j + 1, rows, :] = value.astype(BF)
        if j == 0:
            ref[5, rows, :] = edge(value, -1).astype(BF)
        if j == 3:
            ref[0, rows, :] = edge(value, 1).astype(BF)

    field = lax.broadcasted_iota(jnp.int32, (16, quarter), 0)
    for j in range(4):
        upper = above[j].astype(F32) * top
        lower = below[j].astype(F32) * bottom
        mine = own[j].astype(F32)
        high = jnp.where(field < 8, upper[16:32], mine[0:16])
        low = jnp.where(field < 8, mine[tall - 48 :], lower[0:16])
        keep_phase(
            states, j, slice(0, tall),
            jnp.concatenate([upper[0:16], high, mine[16 : tall - 48], low, lower[16:32]], axis=0),
        )
        tail = jnp.concatenate([upper[24:32], lower[0:8]], axis=0)
        tail = jnp.where(field < 2, 1.0, tail)
        keep_phase(
            ground, j, slice(0, 32), jnp.concatenate([land[j].astype(F32), tail], axis=0)
        )

    for m in range(sources):
        block = coarse[m].astype(F32)
        rows = [block[8 * j : 8 * j + 8] for j in range(quota + 4)]
        rows[1] = top * rows[1] + (1.0 - top) * rows[2]
        rows[quota + 2] = bottom * rows[quota + 2] + (1.0 - bottom) * rows[quota + 1]
        for e in range(ext):
            k, phase = divmod(e - 3, 4)
            j = k + 2
            other, near, far = (
                (j - 1, 0.625, 0.375), (j - 1, 0.875, 0.125), (j + 1, 0.875, 0.125), (j + 1, 0.625, 0.375),
            )[phase]
            value = near * rows[j] + far * rows[other]
            if e < 3:
                value = value * top
            if e >= band + 3:
                value = value * bottom
            rows_of[8 * e : 8 * e + 8, m * LANES : (m + 1) * LANES] = value
    centre = rows_of[...]
    lane = lax.broadcasted_iota(jnp.int32, centre.shape, 1)
    before = jnp.where(lane == 0, centre, pltpu.roll(centre, 1, 1))
    after = jnp.where(lane == quarter - 1, centre, pltpu.roll(centre, quarter - 1, 1))
    for j, (side, near, far) in enumerate(
        ((before, 0.625, 0.375), (before, 0.875, 0.125), (after, 0.875, 0.125), (after, 0.625, 0.375))
    ):
        keep_phase(lifted, j, slice(0, tall), near * centre + far * side)

    done = 0
    for b, s in enumerate(starts_of(band + 4, ROWS1)):
        for j in range(4):
            window = slice(8 * s, 8 * (s + ROWS1 + 2))
            operand = [ground[j], ground[j + 1], ground[j + 2], ground[j + 1]]
            operand += [states[j + k, window] for k in range(3)]
            operand += [lifted[j + k, window] for k in range(3)]
            value = jnp.dot(
                first_two[b, 32 * (done - s) :, :], jnp.concatenate(operand, axis=0),
                preferred_element_type=F32,
            )
            value = silu(value)
            parts = []
            for i in range(done, s + ROWS1):
                part = value[32 * (i - done) : 32 * (i - done) + 32]
                if i < 2:
                    part = part * top
                if i >= band + 2:
                    part = part * bottom
                parts.append(part)
            keep_phase(hidden, j, slice(32 * done, 32 * (s + ROWS1)), jnp.concatenate(parts, axis=0))
        done = s + ROWS1

    done = 0
    for s in starts_of(band + 2, ROWS2):
        for j in range(4):
            window = slice(32 * s, 32 * (s + ROWS2 + 2))
            value = jnp.dot(
                mid_two[...], jnp.concatenate([hidden[j + k, window] for k in range(3)], axis=0),
                preferred_element_type=F32,
            )
            for i in range(done, s + ROWS2):
                rows = slice(32 * (i + 1), 32 * (i + 2))
                part = value[32 * (i - s) : 32 * (i - s) + 32] + hidden[j + 1, rows].astype(F32)
                if i < 1:
                    part = part * top
                if i >= band + 1:
                    part = part * bottom
                summed[j, 32 * i : 32 * i + 32] = part.astype(BF)
        done = s + ROWS2

    high = 8 * ROWS3
    bring.wait()
    sends = []
    for s in range(0, band, ROWS3):
        made = [
            jnp.dot(last_two[...], summed[j, 32 * s : 32 * (s + ROWS3 + 2)], preferred_element_type=F32)
            for j in range(4)
        ]
        west = [edge(made[3][0:high], 1)] + [made[j][0:high] for j in range(3)]
        east = [made[j][2 * high :] for j in range(1, 4)] + [edge(made[0][2 * high :], -1)]
        phases = [west[j] + made[j][high : 2 * high] + east[j] for j in range(4)]
        value = jnp.concatenate(
            [
                jnp.concatenate([p[:, m * LANES : (m + 1) * LANES] for p in phases], axis=1)
                for m in range(sources)
            ],
            axis=0,
        )
        back_all = jnp.dot(value.astype(BF), back[...], preferred_element_type=F32)
        for m in range(sources):
            noise = back_all[m * high : (m + 1) * high]
            cols = slice(4 * LANES * m, 4 * LANES * (m + 1))
            for o in range(8):
                rows = slice(s, s + ROWS3)
                part = noise[ROWS3 * o : ROWS3 * o + ROWS3]
                noise_two[o, rows, cols] = part
                fine_next[o, rows, cols] = keep * fine[o, rows, cols] + blend * part
            if m % 2 == 1:
                there = (slice(None), pl.ds(s, ROWS3), pl.ds(4 * LANES * (m - 1), 8 * LANES))
                for near, far in ((noise_two, noise_far), (fine_next, fine_far_next)):
                    sem = sems.at[1 + len(sends)]
                    sends.append(pltpu.make_async_copy(near.at[there], far.at[there], sem))
                    sends[-1].start()
    for send in sends:
        send.wait()


def turn_matrix():
    made = np.zeros((4 * LANES, 4 * LANES))
    for n in range(4 * LANES):
        made[n, (n % 4) * LANES + n // 4] = 1
    return made


def order_matrix(band):
    made = np.zeros((80 + 8 * (band + 2), 9 * band))
    for o in range(8):
        for y in range(3):
            made[8 * y + o, o * band + band - 3 + y] = 1
            made[32 + 8 * (y + 1) + o, o * band + y] = 1
        for y in range(band):
            made[80 + 8 * (y + 1) + o, o * band + y] = 1
    for y in range(8):
        made[24 + y, 8 * band + band - 8 + y] = 1
        made[32 + y, 8 * band + y] = 1
    for y in range(band):
        made[64 + y, 8 * band + y] = 1
    return made


def body(
    step_index, coarse_state, coarse_forcing, fine_state, land_mask, inlet_one, timing_one, scale_one,
    middle_one, outlet_one, inlet_two, timing_two, land_bias, middle_two, outlet_two,
):
    fields, tile_rows, cols = coarse_state.shape
    _, band, width = fine_state.shape
    row_count, col_count = lax.axis_size("row"), lax.axis_size("col")
    count = row_count * col_count
    state = coarse_state.reshape(fields * tile_rows, cols)
    forcing = coarse_forcing.reshape(fields * tile_rows, cols)
    fine = fine_state.reshape(fields * band, width)
    quarter = width // 4
    ladder = ladder_rows(timing_one.shape[0])

    comb, first_rows, last_rows = pl.pallas_call(
        functools.partial(pack_kernel, tile_rows),
        out_shape=(
            jax.ShapeDtypeStruct((tile_rows, 2 * fields, cols), BF),
            jax.ShapeDtypeStruct((5, 2 * fields, cols), BF),
            jax.ShapeDtypeStruct((5, 2 * fields, cols), BF),
        ),
        in_specs=[ANY] * 2,
        out_specs=[VMEM] * 3,
        scratch_shapes=[
            pltpu.VMEM((fields * tile_rows, cols), F32),
            pltpu.VMEM((fields * tile_rows, cols), F32),
            pltpu.VMEM((fields * tile_rows, cols), BF),
            pltpu.SemaphoreType.DMA((2,)),
        ],
        compiler_params=params(60),
        name="pack",
    )(state, forcing)
    north = lax.ppermute(last_rows, "row", shift_pairs(row_count, 1))
    south = lax.ppermute(first_rows, "row", shift_pairs(row_count, -1))

    turn = turn_matrix()
    split = 2048
    part = split // 4
    shapes = (8 * (band + 2), 16, 32, 32)
    own, ground, to_next, to_prev = pl.pallas_call(
        sort_kernel,
        grid=(width // split,),
        out_shape=[jax.ShapeDtypeStruct((4, rows, quarter), BF) for rows in shapes],
        in_specs=[
            pl.BlockSpec((fields * band, split), lambda n: (0, n)),
            pl.BlockSpec((band, split), lambda n: (0, n)),
            pl.BlockSpec((4 * LANES, 4 * LANES), lambda n: (0, 0)),
            pl.BlockSpec((80 + 8 * (band + 2), 9 * band), lambda n: (0, 0)),
        ],
        out_specs=[pl.BlockSpec((4, rows, part), lambda n: (0, 0, n)) for rows in shapes],
        compiler_params=params(60),
        name="sort",
    )(fine, land_mask, jnp.asarray(turn, BF), jnp.asarray(order_matrix(band), BF))
    north, to_next, to_prev = lax.optimization_barrier((north, to_next, to_prev))
    deep_rows = -(-(tile_rows + 8) // 6) * LANES
    tile, first_cols, last_cols = pl.pallas_call(
        functools.partial(edge_kernel, tile_rows),
        out_shape=(
            jax.ShapeDtypeStruct((cols, deep_rows), BF),
            jax.ShapeDtypeStruct((EDGE, deep_rows), BF),
            jax.ShapeDtypeStruct((EDGE, deep_rows), BF),
        ),
        in_specs=[VMEM] * 3,
        out_specs=[VMEM] * 3,
        compiler_params=params(8),
        name="edges",
    )(north, comb, south)
    west = lax.ppermute(last_cols, "col", shift_pairs(col_count, 1))
    east = lax.ppermute(first_cols, "col", shift_pairs(col_count, -1))
    turned_inlet, first_cols = lax.optimization_barrier(
        (jnp.transpose(inlet_one, (0, 1, 3, 2)), first_cols)
    )
    first_one, mid_one, last_one, bias = pl.pallas_call(
        coarse_weights,
        out_shape=(
            jax.ShapeDtypeStruct((3, 3 * LANES, 256), BF),
            jax.ShapeDtypeStruct((1536, 256), BF),
            jax.ShapeDtypeStruct((96, 256), BF),
            jax.ShapeDtypeStruct((8, 256), F32),
        ),
        in_specs=[SMEM] + [WHOLE] * 5,
        out_specs=[VMEM] * 4,
        compiler_params=params(60),
        name="coarse_weights",
    )(step_index, ladder, timing_one, turned_inlet, middle_one, outlet_one)
    to_next, to_prev, west, east, bias = lax.optimization_barrier((to_next, to_prev, west, east, bias))
    above = lax.ppermute(to_next, ("row", "col"), shift_pairs(count, 1))
    below = lax.ppermute(to_prev, ("row", "col"), shift_pairs(count, -1))
    blocks = len(starts_of(band + 4, ROWS1))
    deep = LANES + 6 * 8 * (ROWS1 + 2)
    first_two, mid_two, last_two = pl.pallas_call(
        functools.partial(fine_weights, band),
        out_shape=(
            jax.ShapeDtypeStruct((blocks, 32 * ROWS1, deep), BF),
            jax.ShapeDtypeStruct((32 * ROWS2, 768), BF),
            jax.ShapeDtypeStruct((24 * ROWS3, 32 * (ROWS3 + 2)), BF),
        ),
        in_specs=[SMEM] + [WHOLE] * 6,
        out_specs=[VMEM] * 3,
        scratch_shapes=[
            pltpu.VMEM((32 * ROWS1, deep - LANES), F32),
            pltpu.VMEM((32 * ROWS2, 768), F32),
            pltpu.VMEM((24 * ROWS3, 32 * (ROWS3 + 2)), F32),
        ],
        compiler_params=params(60),
        name="fine_weights",
    )(step_index, ladder, timing_two, inlet_two, middle_two, outlet_two, land_bias[:, None])

    px = cols + 2 * MARGIN
    pairs = (tile_rows + 8) // 2
    each = tile_rows // col_count
    coarse_next, noise_one, sends = pl.pallas_call(
        functools.partial(coarse_kernel, tile_rows, cols, col_count),
        out_shape=(
            jax.ShapeDtypeStruct((fields * tile_rows, cols), F32),
            jax.ShapeDtypeStruct((fields * tile_rows, cols), F32),
            jax.ShapeDtypeStruct((col_count, (each + 4) * fields, cols), BF),
        ),
        in_specs=[SMEM] + [VMEM] * 11,
        out_specs=[VMEM] * 3,
        scratch_shapes=[
            pltpu.VMEM((-(-pairs // 3), px, 3 * LANES), BF),
            pltpu.VMEM((pairs, px, 256), BF),
            pltpu.VMEM((pairs, px, 768), BF),
            pltpu.VMEM((pairs - 1, px, 256), BF),
            pltpu.VMEM((pairs - 1, 96, px), F32),
        ],
        compiler_params=params(60),
        name="coarse",
    )(
        step_index, north, south, tile, west, east, state, first_one, mid_one, last_one, bias,
        scale_one[None, :],
    )

    arrived = lax.all_to_all(sends, "col", split_axis=0, concat_axis=0, tiled=True)

    fine_next, noise_two = pl.pallas_call(
        functools.partial(fine_kernel, band, quarter),
        out_shape=(
            jax.ShapeDtypeStruct((fields, band, width), F32),
            jax.ShapeDtypeStruct((fields, band, width), F32),
        ),
        in_specs=[SMEM] + [VMEM, ANY] + [VMEM] * 8,
        out_specs=[ANY] * 2,
        scratch_shapes=[
            pltpu.VMEM(((band + 6) * 8, quarter), F32),
            pltpu.VMEM((6, (band + 6) * 8, quarter), BF),
            pltpu.VMEM((6, (band + 6) * 8, quarter), BF),
            pltpu.VMEM((6, 32, quarter), BF),
            pltpu.VMEM((6, (band + 4) * 32, quarter), BF),
            pltpu.VMEM((4, (band + 2) * 32, quarter), BF),
            pltpu.VMEM((fields, band, width), F32),
            pltpu.VMEM((fields, band, width), F32),
            pltpu.VMEM((fields, band, width), F32),
            pltpu.SemaphoreType.DMA((1 + (band // ROWS3) * (quarter // LANES),)),
        ],
        compiler_params=params(60),
        name="fine",
    )(
        step_index, arrived, fine_state, own, ground, above, below, jnp.asarray(turn.T, BF),
        first_two, mid_two, last_two,
    )

    return (
        coarse_next.reshape(coarse_state.shape),
        noise_one.reshape(coarse_state.shape),
        fine_next,
        noise_two,
    )


def solution(mesh):
    return jax.shard_map(
        body,
        mesh=mesh,
        in_specs=(
            P(), P(None, "row", "col"), P(None, "row", "col"), P(None, ("row", "col"), None),
            P(("row", "col"), None), P(), P(), P(), P(), P(), P(), P(), P(), P(), P(),
        ),
        out_specs=(
            P(None, "row", "col"), P(None, "row", "col"), P(None, ("row", "col"), None),
            P(None, ("row", "col"), None),
        ),
        check_vma=False,
    )
```
